512 devices in a mesh: dp: 2 (over core), seq: 32 (over x, y), tensor: 8 (over z).
Axes of the slice: x: 4, y: 8, z: 8, core: 2. Of those that a mesh axis runs over, the one named last changes fastest.
Arguments:
- query: bfloat16 [512, 8192], P(('dp', 'seq'), 'tensor'), may hold values from -40 to 40
- fresh_key_value: bfloat16 [512, 2, 1024], P(('dp', 'seq'), None, 'tensor'), may hold values from -6 to 6
- cache: bfloat16 [512, 256, 2, 1024], P(('dp', 'seq'), None, None, 'tensor'), may hold values from -20 to 20
- lengths: int32 [512], P(('dp', 'seq')), may hold values from 2 to 256
- destination: int32 [512, 1], P(('dp', 'tensor')), may hold values from 0 to 32; in each aligned block of 32 rows (0 to 31, 32 to 63, ...) at most 2 rows name the same one
- out_weight: bfloat16 [8192, 8192], P('tensor', 'seq'), may hold values from -0.0625 to 0.0625
- learner_ctx: bfloat16 [8192, 8192], P(('dp', 'seq'), 'tensor'), may hold values from -6 to 6
Outputs:
- decoded: bfloat16 [512, 8192], P(('dp', 'tensor'), 'seq')
- handed: bfloat16 [2, 32, 8, 2, 8192], P('dp', 'seq', 'tensor')
- recomputed: bfloat16 [8192, 8192], P(('dp', 'tensor'), 'seq')
The draws below stay inside these ranges and needn't reach their ends.
Inputs may be any that keep to these rules, and one draw needn't show every extreme that they name: In each block of 32 projected rows no destination is named by more than 2 rows, and some destination reaches 2.
All inputs are finite; a program needn't handle non-finite values.
Results may differ from the reference program's by a relative error of at most 0.017.
Values may be sent and summed in bfloat16 or wider, within the bound.
A program may use at most 64 MiB of HBM per device.

```python
import math
import jax
import jax.numpy as jnp
import numpy as np
from jax import lax

D = 8192
QUERY_HEADS = 64
KEY_VALUE_HEADS = 8
HEAD_SIZE = 128
CACHED_POSITIONS = 256
ROLLOUT_ROWS = 512
SROWS = 32
CAP = 2
LTOK = 8192
N_DP = 2
N_SEQ = 32
N_TENSOR = 8


def draw_cache(key, part):
    key = jax.random.fold_in(key, 11)
    start_offset = jnp.clip(jax.random.normal(key, (ROLLOUT_ROWS, CACHED_POSITIONS, 2, KEY_VALUE_HEADS * HEAD_SIZE), jnp.float32), -5.0, 5.0)
    return start_offset.astype(jnp.bfloat16)


def draw_query(key, part):
    key = jax.random.fold_in(key, 12)
    start_offset = jnp.clip(jax.random.normal(key, (ROLLOUT_ROWS, QUERY_HEADS * HEAD_SIZE), jnp.float32), -5.0, 5.0)
    return start_offset.astype(jnp.bfloat16)


def set_ends(values, key, smallest, high):
    longest = values.shape.index(max(values.shape))
    spots = []
    for shift in (0, 1):
        where = [jax.random.randint(jax.random.fold_in(key, axis), (), 0, length) for axis, length in enumerate(values.shape)]
        where[longest] = (where[longest] + shift) % values.shape[longest]
        spots.append(tuple(where))
    return values.at[spots[0]].set(smallest).at[spots[1]].set(high)


def steps_of(stream_key, shape, cuts, smallest, largest):
    factor_of, own = 1.0, jax.random.fold_in(stream_key, 6)
    for axis_at, blocks in cuts:
        draws = jnp.exp(jax.random.uniform(jax.random.fold_in(own, axis_at), (blocks,), jnp.float32, smallest / len(cuts), largest / len(cuts)))
        factor_of = factor_of * jnp.repeat(draws, shape[axis_at] // blocks).reshape([-1 if axis == axis_at else 1 for axis in range(len(shape))])
    return factor_of


def deal_out(key, own, number, rows, number_of, top, limit, skew):
    sequence = jax.random.permutation(key, number_of)
    crowded, ordinary = shares(number_of, rows * top, limit, skew, True), shares(number_of, rows * top, limit, skew, False)
    places = jnp.arange(number_of)

    def named(sizes, turn):
        used = int((sizes > 0).sum())
        fixed = max(1, used // 4)
        passed = fixed + (places - fixed + turn * (used - fixed)) % max(1, number_of - fixed)
        return jnp.zeros((number_of,), jnp.int32).at[sequence[jnp.where(places < fixed, places, passed)]].set(jnp.asarray(sizes, jnp.int32))

    sizes = jnp.where(number % 4 == 0, named(crowded, number // 4), named(ordinary, number - number // 4 - 1))
    mixed = jax.random.permutation(jax.random.fold_in(own, 3), number_of)
    source_of, sink = mixed[0:number_of // 2 * 2:2], mixed[1:number_of // 2 * 2:2]
    margin = jnp.minimum(sizes[source_of] - 1, limit - sizes[sink]) // 2
    margin = jnp.where((source_of == sequence[0]) | (sink == sequence[0]) | (sizes[sink] == 0), 0, jnp.maximum(margin, 0))
    passed = jax.random.randint(jax.random.fold_in(own, 4), (number_of // 2,), 0, 1 << 20) % (margin + 1)
    sizes = sizes.at[source_of].add(-passed).at[sink].add(passed)
    labels = jnp.searchsorted(jnp.cumsum(sizes), jnp.arange(rows * top), side="right").astype(jnp.int32)
    table = labels.reshape(top, rows).T
    table = table[jax.random.permutation(jax.random.fold_in(own, 1), rows)]
    turn = jax.random.randint(jax.random.fold_in(own, 2), (rows, 1), 0, top)
    return jnp.take_along_axis(table, (jnp.arange(top)[None, :] + turn) % top, axis=1)


def shares(count, total, bound, skew, full):
    weights = [(1 << 20) // math.isqrt(rank ** skew) + 1 for rank in range(1, count + 1)]
    largest = bound if full else min(bound, max(-(-total // count), total * weights[0] // sum(weights)))
    least = 1 if total - largest >= count - 1 else 0
    counts, rest = [largest] + [least] * (count - 1), total - largest - least * (count - 1)
    while rest > 0:
        free = [i for i in range(1, count) if counts[i] < largest] or [i for i in range(1, count) if counts[i] < bound]
        whole, left = sum([weights[i] for i in free]), rest
        for i in free:
            more = min(bound - counts[i], max(1, left * weights[i] // whole), rest)
            counts[i] = counts[i] + more
            rest = rest - more
    return np.array(counts)


def normal_values(stream_key, shape, deviation, most, shards=(), kind=jnp.bfloat16):
    drawn = jax.random.normal(stream_key, shape, jnp.float32) * deviation
    if len(shards) > 0:
        drawn = steps_of(stream_key, shape, shards, -0.22, 0.18) * drawn
    return jnp.clip(drawn, min=-most, max=most).astype(kind)


def setup_inputs(seed: int = 0) -> dict:
    key_of = jax.random.split(jax.random.key(seed), 8)
    query = draw_query(jax.random.fold_in(key_of[7], 71), 0)
    fresh_key_value = normal_values(key_of[1], (ROLLOUT_ROWS, 2, KEY_VALUE_HEADS * HEAD_SIZE), 1.0, 6.0, ((0, 64), (2, 8)))
    cache = draw_cache(jax.random.fold_in(key_of[7], 71), 0)
    lengths = set_ends(jax.random.randint(key_of[3], (ROLLOUT_ROWS,), 2, CACHED_POSITIONS + 1), jax.random.fold_in(key_of[3], 1), 2, CACHED_POSITIONS).astype(jnp.int32)
    destination_keys = jax.random.split(jax.random.fold_in(key_of[4], 1), ROLLOUT_ROWS // SROWS)
    destination_turns = jax.random.permutation(jax.random.fold_in(key_of[4], 3), ROLLOUT_ROWS // SROWS)
    destination = jax.vmap(lambda own, number: deal_out(jax.random.fold_in(key_of[4], 2), own, number, SROWS, N_SEQ + 1, 1, CAP, 2))(destination_keys, destination_turns).reshape((ROLLOUT_ROWS, 1))
    out_weight = normal_values(key_of[5], (QUERY_HEADS * HEAD_SIZE, D), (QUERY_HEADS * HEAD_SIZE) ** -0.5, 0.0625, ((0, 8), (1, 32)))
    learner_ctx = normal_values(key_of[6], (LTOK, QUERY_HEADS * HEAD_SIZE), 1.0, 6.0, ((0, 64), (1, 8)))
    return {"query": query, "fresh_key_value": fresh_key_value, "cache": cache, "lengths": lengths, "destination": destination, "out_weight": out_weight, "learner_ctx": learner_ctx}


def attend_row(item):
    query_rows, self_key_value, cache_entries, length = item
    query_group = QUERY_HEADS // KEY_VALUE_HEADS
    score_scale = HEAD_SIZE ** -0.5
    head_list = query_rows.astype(jnp.float32).reshape(KEY_VALUE_HEADS, query_group, HEAD_SIZE)
    rows_of_keys = cache_entries[:, 0].astype(jnp.float32).reshape(CACHED_POSITIONS, KEY_VALUE_HEADS, HEAD_SIZE)
    rows_of_values = cache_entries[:, 1].astype(jnp.float32).reshape(CACHED_POSITIONS, KEY_VALUE_HEADS, HEAD_SIZE)
    self_key = self_key_value[0].astype(jnp.float32).reshape(KEY_VALUE_HEADS, HEAD_SIZE)
    self_value = self_key_value[1].astype(jnp.float32).reshape(KEY_VALUE_HEADS, HEAD_SIZE)
    scores = jnp.einsum('gjd,pgd->gjp', head_list, rows_of_keys) * score_scale
    own = jnp.einsum('gjd,gd->gj', head_list, self_key) * score_scale
    valid = jnp.arange(CACHED_POSITIONS) < length
    scores = jnp.where(valid[None, None, :], scores, -jnp.inf)
    top = jnp.maximum(jnp.max(scores, axis=-1), own)
    expd = jnp.exp(scores - top[..., None])
    own_exp = jnp.exp(own - top)
    total = jnp.sum(expd, axis=-1) + own_exp
    weights = lax.optimization_barrier((expd / total[..., None]).astype(jnp.bfloat16)).astype(jnp.float32)
    own_weight = lax.optimization_barrier((own_exp / total).astype(jnp.bfloat16)).astype(jnp.float32)
    context = jnp.einsum('gjp,pgd->gjd', weights, rows_of_values) + own_weight[..., None] * self_value[:, None, :]
    return context.reshape(QUERY_HEADS * HEAD_SIZE).astype(jnp.bfloat16)


def reference(query, fresh_key_value, cache, lengths, destination, out_weight, learner_ctx):
    context = lax.map(attend_row, (query, fresh_key_value, cache, lengths))
    decoded = jnp.dot(context, out_weight, preferred_element_type=jnp.float32).astype(jnp.bfloat16)
    target = destination[:, 0]
    onehot = (target[:, None] == jnp.arange(N_SEQ + 1)[None, :]).astype(jnp.int32)
    block_count = ROLLOUT_ROWS // SROWS
    ranks = jnp.cumsum(onehot.reshape(block_count, SROWS, N_SEQ + 1), axis=1).reshape(ROLLOUT_ROWS, N_SEQ + 1) - 1
    my_rank = jnp.sum(ranks * onehot, axis=1).astype(jnp.int32)
    block_of = jnp.arange(ROLLOUT_ROWS, dtype=jnp.int32) // SROWS
    handed = jnp.zeros((N_DP, N_SEQ, N_TENSOR, CAP, D), jnp.bfloat16)
    handed = handed.at[block_of // N_TENSOR, target, block_of % N_TENSOR, my_rank].set(decoded, mode='drop')
    width = QUERY_HEADS * HEAD_SIZE // N_TENSOR
    summed = jnp.zeros((LTOK, D), jnp.float32)
    for part in range(N_TENSOR):
        partial_value = jnp.dot(learner_ctx[:, part * width:(part + 1) * width], out_weight[part * width:(part + 1) * width], preferred_element_type=jnp.float32).astype(jnp.bfloat16)
        summed = summed + partial_value.astype(jnp.float32)
    recomputed = summed.astype(jnp.bfloat16)
    return decoded, handed, recomputed
```

```python
import jax
import jax.numpy as jnp
from jax import lax
from jax.experimental import pallas as pl
from jax.experimental.pallas import tpu as pltpu
from jax.sharding import PartitionSpec as P

QUERY_GROUP = 8
HEAD_SIZE = 128
CACHED_POSITIONS = 256
NX, NY, NZ = 4, 8, 8
BLOCK = 128
HALF = 64
WIDTH = 1024
COLS = 256
ITEMS = NY
SLOTS = ITEMS + NZ - 1
OFFSETS = (0, 3, 1, 2)
MESH_ID = pl.DeviceIdType.MESH
BF16, F32 = jnp.bfloat16, jnp.float32


def dot(a, b):
    return jnp.dot(a, b, preferred_element_type=F32)


def dot_t(a, b):
    return lax.dot_general(a, b, (((1,), (1,)), ((), ())), preferred_element_type=F32)


def iota(shape, dim):
    return lax.broadcasted_iota(jnp.int32, shape, dim)


def one_hot(condition):
    return jnp.where(condition, 1.0, 0.0).astype(BF16)


def attend(q_ref, f_ref, c_ref, len_ref):
    rows = 8
    by_head = jnp.concatenate(
        [q_ref[:, h * HEAD_SIZE : (h + 1) * HEAD_SIZE].astype(F32) for h in range(QUERY_GROUP)], axis=0
    ).astype(BF16)
    r64, c64 = iota((64, 64), 0), iota((64, 64), 1)
    swap = one_hot((r64 % 8) * 8 + r64 // 8 == c64)
    queries = dot(swap, by_head)
    scale = HEAD_SIZE ** (-0.5)
    scores = []
    place = iota((8, 2 * CACHED_POSITIONS), 1)
    for r in range(rows):
        s = dot_t(queries[r * 8 : (r + 1) * 8].astype(BF16), c_ref[r]) * scale
        valid = (place % 2 == 0) & (place < 2 * len_ref[r])
        scores.append(jnp.where(valid, s, -1e30))
    scores = jnp.concatenate(scores, axis=0)
    fresh = f_ref[...]
    fresh_scores = dot_t(queries.astype(BF16), fresh) * scale
    row16, col16 = iota((64, 16), 0), iota((64, 16), 1)
    own = jnp.sum(jnp.where(col16 == 2 * (row16 // 8), fresh_scores, 0.0), axis=1, keepdims=True)
    top = jnp.maximum(jnp.max(scores, axis=1, keepdims=True), own)
    expd = jnp.exp(scores - top)
    own_exp = jnp.exp(own - top)
    total = jnp.sum(expd, axis=1, keepdims=True) + own_exp
    weights = pltpu.roll(expd / total, 1, 1)
    own_weight = jnp.where(col16 == 2 * (row16 // 8) + 1, own_exp / total, 0.0).astype(BF16)
    context = [dot(weights[r * 8 : (r + 1) * 8].astype(BF16), c_ref[r]) for r in range(rows)]
    context = jnp.concatenate(context, axis=0) + dot(own_weight, fresh)
    context = dot(swap, context.astype(BF16))
    halves = [
        jnp.concatenate([context[h * 8 : (h + 1) * 8] for h in range(g * 4, g * 4 + 4)], axis=1) for g in (0, 1)
    ]
    return jnp.concatenate(halves, axis=0).astype(BF16)


def placement(dest_ref):
    dest = dest_ref[...].astype(F32)
    r32, c32 = iota((32, 32), 0), iota((32, 32), 1)
    across = jnp.broadcast_to(dest, (32, 32))
    down = dot(jnp.where(r32 == c32, across, 0.0).astype(BF16), jnp.ones((32, 32), BF16))
    earlier = one_hot((down == across) & (r32 < c32))
    rank = dot(jnp.ones((128, 32), BF16), earlier)
    q, i = iota((128, 32), 0), iota((128, 32), 1)
    target = ((q // 4) % 4) * NY + q // 16
    slot = (q // 2) % 2
    hit = (jnp.broadcast_to(dest, (128, 32)) == target.astype(F32)) & (rank == slot.astype(F32))
    return [one_hot(hit & (q % 2 == h)) for h in (0, 1)]


def regroup():
    r, c = iota((128, 128), 0), iota((128, 128), 1)
    return one_hot((r // 4 % 8) * 16 + (r // 32) * 4 + r % 4 == c)


def regroup_last():
    r, c = iota((128, 128), 0), iota((128, 128), 1)
    return one_hot((r // 2 % 32) * 4 + (r // 64) * 2 + r % 2 == c)


def kernel(
    q_ref, f_ref, c_ref, len_ref, dest_ref, w_ref, a_ref,
    dec_ref, hand_ref, rec_ref,
    abuf, wbuf, pbuf, rbuf, sbuf, cbuf, zs, zr, h1s, h1r, h2s, h2r,
    a_send, a_recv, w_send, w_recv, d_send, d_recv, c_send, c_recv, out_recv,
):
    core, seq, z = lax.axis_index("dp"), lax.axis_index("seq"), lax.axis_index("tensor")
    x, y = seq // NY, seq % NY

    def at(dx=0, dy=0, dz=0):
        return {"seq": lax.rem(x + dx + NX, NX) * NY + lax.rem(y + dy + NY, NY), "tensor": lax.rem(z + dz + NZ, NZ)}

    sibling = {"dp": 1 - core}
    partners = (
        [at(dx=k) for k in range(1, NX)] + [at(dy=k) for k in range(1, NY)] + [at(dz=k) for k in range(1, NZ)] + [sibling]
    )

    def send(src, dst, send_sem, recv_sem, device):
        copy = pltpu.make_async_remote_copy(
            src_ref=src, dst_ref=dst, send_sem=send_sem, recv_sem=recv_sem, device_id=device, device_id_type=MESH_ID
        )
        copy.start()

    def wait(ref, sem):
        pltpu.make_async_copy(ref, ref, sem).wait()

    barrier = pltpu.get_barrier_semaphore()
    for device in partners:
        pl.semaphore_signal(barrier, inc=1, device_id=device, device_id_type=MESH_ID)
    abuf[0] = a_ref[...]
    pl.semaphore_wait(barrier, len(partners))

    def half(item, h):
        return abuf.at[item, pl.ds(pl.multiple_of(h * HALF, HALF), HALF)]

    def send_rows(stream, source, target, h):
        send(half(source, h), half(target, h), a_send.at[stream], a_recv.at[stream, target - 1], at(dy=1 - 2 * stream))

    for i in (0, 1):
        for stream in (0, 1):
            send_rows(stream, 0, i + 1, (i + stream) % 2)

    kept = pl.multiple_of(core * (WIDTH // 2), WIDTH // 2)
    mine, other = pl.ds(kept, WIDTH // 2), pl.ds(pl.multiple_of(WIDTH // 2 - kept, WIDTH // 2), WIDTH // 2)
    quarter = [pl.ds(pl.multiple_of(kept + k * (WIDTH // 4), WIDTH // 4), WIDTH // 4) for k in (0, 1)]
    send(w_ref.at[mine], wbuf.at[0, mine], w_send.at[0], w_recv.at[0], at(dx=1))
    send(w_ref.at[mine], wbuf.at[1, mine], w_send.at[0], w_recv.at[1], at(dx=-1))

    cbuf[x, y] = attend(q_ref, f_ref, c_ref, len_ref)
    for k in range(1, NY):
        send(cbuf.at[x, y], cbuf.at[x, y], d_send.at[0], d_recv.at[0], at(dy=k))

    def gather(i):
        for stream in (0, 1):
            h = lax.rem(i + stream, 2)
            wait(half(i + 1, h), a_recv.at[stream, i])

            @pl.when(i < 5)
            def _():
                send_rows(stream, i + 1, i + 3, h)

    gather(0)
    for k in (0, 1):
        wait(wbuf.at[k, mine], w_recv.at[k])
        send(wbuf.at[k, quarter[k]], wbuf.at[2, quarter[k]], w_send.at[0], w_recv.at[2 + k], at(dx=1 - 2 * k))
        send(wbuf.at[k, mine], wbuf.at[k, mine], w_send.at[1], w_recv.at[4 + k], sibling)
    gather(1)
    wait(cbuf.at[x, pl.ds(0, NY - 1)], d_recv.at[0])
    for k in range(1, NX):
        send(cbuf.at[x], cbuf.at[x], d_send.at[1], d_recv.at[1], at(dx=k))
    gather(2)
    for k in (0, 1):
        wait(wbuf.at[2, quarter[k]], w_recv.at[2 + k])
    send(wbuf.at[2, mine], wbuf.at[2, mine], w_send.at[1], w_recv.at[6], sibling)
    for j in range(3):
        wait(wbuf.at[j, other], w_recv.at[4 + j])

    def chain(s, way, root):
        tz = 2 * x + root
        place = lax.rem(z - tz - 1 + 2 * NZ, NZ) if way == 0 else lax.rem(tz - 1 - z + 2 * NZ, NZ)
        m = s - place
        k = (m + 1) // 2
        item_y = lax.rem(y + 2 * NY + jnp.where(lax.rem(m + 1 + NZ, 2) == way, -k, k), NY)

        @pl.when((m >= 0) & (m < ITEMS) & (item_y // 4 == root))
        def _():
            for j in range(NX):
                own = pbuf.at[m, j, pl.ds(way * HALF, HALF)]

                @pl.when(place == 0)
                def _():
                    sbuf[way, m, j] = own[...].astype(BF16)

                @pl.when(place > 0)
                def _():
                    wait(rbuf.at[way, m, j], c_recv.at[way, m, j])
                    sbuf[way, m, j] = (own[...] + rbuf[way, m, j].astype(F32)).astype(BF16)

                @pl.when(place < NZ - 1)
                def _():
                    send(
                        sbuf.at[way, m, j], rbuf.at[way, m, j], c_send.at[way], c_recv.at[way, m, j],
                        at(dz=1 - 2 * way),
                    )

                @pl.when(place == NZ - 1)
                def _():
                    rows = pl.ds(pl.multiple_of(lax.rem(item_y, 4) * BLOCK + way * HALF, HALF), HALF)
                    if j == 0:
                        pltpu.make_async_copy(sbuf.at[way, m, j], rec_ref.at[rows], c_send.at[way]).start()
                    else:
                        send(sbuf.at[way, m, j], rec_ref.at[rows], c_send.at[way], out_recv.at[0], at(dx=OFFSETS[j]))

    def project_decode():
        wait(cbuf.at[pl.ds(0, NX - 1)], d_recv.at[1])
        for g in range(NX):
            rows = cbuf[g].reshape(NY * 16, 512)
            low = dot(rows, w_ref[0:512]).reshape(NY, 16, COLS)
            high = dot(rows, w_ref[512:1024]).reshape(NY, 16, COLS)
            zs[2 * g : 2 * g + 2] = (low[:, :8] + high[:, 8:]).reshape(2, 32, COLS).astype(BF16)
        zr[z] = zs[z]
        for k in range(1, NZ):
            send(zs.at[lax.rem(z + k, NZ)], zr.at[z], d_send.at[2], d_recv.at[2], at(dz=k))

    def hand_over():
        wait(zr.at[pl.ds(0, NZ - 1)], d_recv.at[2])
        total = zr[0].astype(F32)
        for k in range(1, NZ):
            total = total + zr[k].astype(F32)
        decoded = total.astype(BF16)
        dec_ref[...] = decoded
        maps = placement(dest_ref)
        out = dot(maps[0], decoded[:, :128]) + dot(maps[1], decoded[:, 128:])
        h1s[...] = out.astype(BF16).reshape(NY, 16, 128)
        h1r[y] = h1s[y]
        for k in range(1, NY):
            send(h1s.at[lax.rem(y + k, NY)], h1r.at[y], d_send.at[3], d_recv.at[3], at(dy=k))

    def hand_on():
        wait(h1r.at[pl.ds(0, NY - 1)], d_recv.at[3])
        h2s[...] = dot(regroup(), h1r[...].reshape(128, 128)).astype(BF16).reshape(NX, 32, 128)
        h2r[x] = h2s[x]
        for k in range(1, NX):
            send(h2s.at[lax.rem(x + k, NX)], h2r.at[x], d_send.at[4], d_recv.at[4], at(dx=k))

    def take():
        wait(h2r.at[pl.ds(0, NX - 1)], d_recv.at[4])
        hand_ref[...] = dot(regroup_last(), h2r[...].reshape(128, 128)).astype(BF16)

    def slot(s, carry):
        @pl.when((s >= 4) & (s < ITEMS))
        def _():
            gather(s - 1)

        @pl.when(s < ITEMS)
        def _():
            rows = abuf[s]
            for j in range(NX):
                pbuf[s, j] = dot(rows, w_ref[...] if j == 0 else wbuf[j - 1])

        for way in (0, 1):
            for root in (0, 1):
                chain(s, way, root)
        for step, task in ((3, project_decode), (5, hand_over), (7, hand_on), (9, take)):
            pl.when(s == step)(task)
        return carry

    lax.fori_loop(0, SLOTS, slot, 0)

    @pl.when(x != z // 2)
    def _():
        wait(rec_ref, out_recv.at[0])

    for way in (0, 1):
        wait(sbuf.at[way], c_send.at[way])
        wait(abuf.at[pl.ds(0, 7), pl.ds(0, HALF)], a_send.at[way])
    wait(wbuf.at[pl.ds(0, 2), mine], w_send.at[0])
    for k in (0, 1):
        wait(wbuf.at[k, quarter[k]], w_send.at[0])
    wait(wbuf.at[:, mine], w_send.at[1])
    wait(cbuf.at[0, pl.ds(0, NY - 1)], d_send.at[0])
    wait(cbuf.at[pl.ds(0, NX - 1)], d_send.at[1])
    wait(zs.at[pl.ds(0, NZ - 1)], d_send.at[2])
    wait(h1s.at[pl.ds(0, NY - 1)], d_send.at[3])
    wait(h2s.at[pl.ds(0, NX - 1)], d_send.at[4])


def local(query, fresh_key_value, cache, lengths, destination, out_weight, learner_ctx):
    vmem = pl.BlockSpec(memory_space=pltpu.VMEM)
    dma = pltpu.SemaphoreType.DMA
    decoded, handed, recomputed = pl.pallas_call(
        kernel,
        out_shape=(
            jax.ShapeDtypeStruct((32, COLS), BF16),
            jax.ShapeDtypeStruct((128, 128), BF16),
            jax.ShapeDtypeStruct((512, COLS), BF16),
        ),
        in_specs=[vmem, vmem, vmem, pl.BlockSpec(memory_space=pltpu.SMEM), vmem, vmem, vmem],
        out_specs=(vmem, vmem, vmem),
        scratch_shapes=[
            pltpu.VMEM((ITEMS, BLOCK, WIDTH), BF16),
            pltpu.VMEM((NX - 1, WIDTH, COLS), BF16),
            pltpu.VMEM((ITEMS, NX, BLOCK, COLS), F32),
            pltpu.VMEM((2, ITEMS, NX, HALF, COLS), BF16),
            pltpu.VMEM((2, ITEMS, NX, HALF, COLS), BF16),
            pltpu.VMEM((NX, NY, 16, 512), BF16),
            pltpu.VMEM((NZ, 32, COLS), BF16),
            pltpu.VMEM((NZ, 32, COLS), BF16),
            pltpu.VMEM((NY, 16, 128), BF16),
            pltpu.VMEM((NY, 16, 128), BF16),
            pltpu.VMEM((NX, 32, 128), BF16),
            pltpu.VMEM((NX, 32, 128), BF16),
            dma((2,)),
            dma((2, 7)),
            dma((2,)),
            dma((7,)),
            dma((5,)),
            dma((5,)),
            dma((2,)),
            dma((2, ITEMS, NX)),
            dma((1,)),
        ],
        compiler_params=pltpu.CompilerParams(
            collective_id=0, has_side_effects=True, vmem_limit_bytes=48 * 1024 * 1024
        ),
        cost_estimate=pl.CostEstimate(flops=2300000000, bytes_accessed=2500000, transcendentals=33000),
        name="project",
    )(
        query,
        fresh_key_value.reshape(16, HEAD_SIZE),
        cache.reshape(8, 2 * CACHED_POSITIONS, HEAD_SIZE),
        lengths,
        destination.reshape(1, 32),
        out_weight,
        learner_ctx,
    )
    return decoded, handed.reshape(1, 1, 1, 2, 8192), recomputed


def solution(mesh):
    return jax.shard_map(
        local,
        mesh=mesh,
        in_specs=(
            P(("dp", "seq"), "tensor"),
            P(("dp", "seq"), None, "tensor"),
            P(("dp", "seq"), None, None, "tensor"),
            P(("dp", "seq")),
            P(("dp", "tensor"), None),
            P("tensor", "seq"),
            P(("dp", "seq"), "tensor"),
        ),
        out_specs=(
            P(("dp", "tensor"), "seq"),
            P("dp", "seq", "tensor", None, None),
            P(("dp", "tensor"), "seq"),
        ),
        check_vma=False,
    )
```

```python
import jax
import jax.numpy as jnp
from jax import lax
from jax.experimental import pallas as pl
from jax.experimental.pallas import tpu as pltpu
from jax.sharding import PartitionSpec as P

QUERY_GROUP = 8
HEAD_SIZE = 128
CACHED_POSITIONS = 256
NX, NY, NZ = 4, 8, 8
BLOCK = 128
HALF = 64
WIDTH = 1024
COLS = 256
ITEMS = NY
CHUNKS = [(0, 0), (1, 0), (2, 0), (0, 1), (0, 2), (1, 1), (1, 2), (2, 1), (2, 2), (3, 0), (3, 1), (3, 2)]
CHUNKS += [(m, 3) for m in range(4)] + [(m, j) for m in range(4, ITEMS) for j in range(NX)]
ROUNDS = 8
MESH_ID = pl.DeviceIdType.MESH
BF16, F32 = jnp.bfloat16, jnp.float32


def dot(a, b):
    return jnp.dot(a, b, preferred_element_type=F32)


def dot_t(a, b):
    return lax.dot_general(a, b, (((1,), (1,)), ((), ())), preferred_element_type=F32)


def iota(shape, dim):
    return lax.broadcasted_iota(jnp.int32, shape, dim)


def one_hot(condition):
    return jnp.where(condition, 1.0, 0.0).astype(BF16)


def attend(q_ref, f_ref, c_ref, len_ref):
    rows = 8
    by_head = jnp.concatenate(
        [q_ref[:, h * HEAD_SIZE : (h + 1) * HEAD_SIZE].astype(F32) for h in range(QUERY_GROUP)], axis=0
    ).astype(BF16)
    r64, c64 = iota((64, 64), 0), iota((64, 64), 1)
    swap = one_hot((r64 % 8) * 8 + r64 // 8 == c64)
    queries = dot(swap, by_head)
    scale = HEAD_SIZE ** (-0.5)
    scores = []
    place = iota((8, 2 * CACHED_POSITIONS), 1)
    for r in range(rows):
        s = dot_t(queries[r * 8 : (r + 1) * 8].astype(BF16), c_ref[r]) * scale
        valid = (place % 2 == 0) & (place < 2 * len_ref[r])
        scores.append(jnp.where(valid, s, -1e30))
    scores = jnp.concatenate(scores, axis=0)
    fresh = f_ref[...]
    fresh_scores = dot_t(queries.astype(BF16), fresh) * scale
    row16, col16 = iota((64, 16), 0), iota((64, 16), 1)
    own = jnp.sum(jnp.where(col16 == 2 * (row16 // 8), fresh_scores, 0.0), axis=1, keepdims=True)
    top = jnp.maximum(jnp.max(scores, axis=1, keepdims=True), own)
    expd = jnp.exp(scores - top)
    own_exp = jnp.exp(own - top)
    total = jnp.sum(expd, axis=1, keepdims=True) + own_exp
    weights = pltpu.roll(expd / total, 1, 1)
    own_weight = jnp.where(col16 == 2 * (row16 // 8) + 1, own_exp / total, 0.0).astype(BF16)
    context = [dot(weights[r * 8 : (r + 1) * 8].astype(BF16), c_ref[r]) for r in range(rows)]
    context = jnp.concatenate(context, axis=0) + dot(own_weight, fresh)
    context = dot(swap, context.astype(BF16))
    halves = [
        jnp.concatenate([context[h * 8 : (h + 1) * 8] for h in range(g * 4, g * 4 + 4)], axis=1) for g in (0, 1)
    ]
    return jnp.concatenate(halves, axis=0).astype(BF16)


def placement(dest_ref):
    dest = dest_ref[...].astype(F32)
    r32, c32 = iota((32, 32), 0), iota((32, 32), 1)
    across = jnp.broadcast_to(dest, (32, 32))
    down = dot(jnp.where(r32 == c32, across, 0.0).astype(BF16), jnp.ones((32, 32), BF16))
    earlier = one_hot((down == across) & (r32 < c32))
    rank = dot(jnp.ones((128, 32), BF16), earlier)
    q, i = iota((128, 32), 0), iota((128, 32), 1)
    target = ((q // 4) % 4) * NY + q // 16
    slot = (q // 2) % 2
    hit = (jnp.broadcast_to(dest, (128, 32)) == target.astype(F32)) & (rank == slot.astype(F32))
    return [one_hot(hit & (q % 2 == h)) for h in (0, 1)]


def regroup():
    r, c = iota((128, 128), 0), iota((128, 128), 1)
    return one_hot((r // 4 % 8) * 16 + (r // 32) * 4 + r % 4 == c)


def regroup_last():
    r, c = iota((128, 128), 0), iota((128, 128), 1)
    return one_hot((r // 2 % 32) * 4 + (r // 64) * 2 + r % 2 == c)


def kernel(
    q_hbm, f_hbm, c_hbm, len_hbm, dest_hbm, w_hbm, a_hbm,
    dec_ref, hand_ref, rec_ref,
    q_ref, f_ref, c_ref, len_ref, dest_ref,
    abuf, wbuf, pbuf, rbuf, sbuf, cbuf, zs, zr, h1s, h1r, h2s, h2r,
    in_sem, a_send, a_recv, w_send, w_recv, d_send, d_recv, c_send, c_recv, f_send, out_recv,
):
    core, seq, z = lax.axis_index("dp"), lax.axis_index("seq"), lax.axis_index("tensor")
    x, y = seq // NY, seq % NY

    def at(dx=0, dy=0, dz=0):
        return {"seq": lax.rem(x + dx + NX, NX) * NY + lax.rem(y + dy + NY, NY), "tensor": lax.rem(z + dz + NZ, NZ)}

    sibling = {"dp": 1 - core}
    partners = (
        [at(dx=k) for k in range(1, NX)] + [at(dy=k) for k in range(1, NY)] + [at(dz=k) for k in range(1, NZ)] + [sibling]
    )

    def send(src, dst, send_sem, recv_sem, device):
        copy = pltpu.make_async_remote_copy(
            src_ref=src, dst_ref=dst, send_sem=send_sem, recv_sem=recv_sem, device_id=device, device_id_type=MESH_ID
        )
        copy.start()

    def wait(ref, sem):
        pltpu.make_async_copy(ref, ref, sem).wait()

    barrier = pltpu.get_barrier_semaphore()
    for device in partners:
        pl.semaphore_signal(barrier, inc=1, device_id=device, device_id_type=MESH_ID)
    loads = [
        pltpu.make_async_copy(src, dst, in_sem.at[k])
        for k, (src, dst) in enumerate(
            [
                (a_hbm, abuf.at[0]), (w_hbm, wbuf.at[:, pl.ds(0, COLS)]), (q_hbm, q_ref), (c_hbm, c_ref),
                (f_hbm, f_ref), (len_hbm, len_ref), (dest_hbm, dest_ref),
            ]
        )
    ]
    for load in loads:
        load.start()
    for load in loads:
        load.wait()
    pl.semaphore_wait(barrier, len(partners))

    def half(item, h):
        return abuf.at[item, pl.ds(pl.multiple_of(h * HALF, HALF), HALF)]

    def send_rows(stream, source, target, h):
        send(half(source, h), half(target, h), a_send.at[stream], a_recv.at[stream, target - 1], at(dy=1 - 2 * stream))

    for i in (0, 1):
        for stream in (0, 1):
            send_rows(stream, 0, i + 1, (i + stream) % 2)

    def gather(i):
        for stream in (0, 1):
            h = (i + stream) % 2
            wait(half(i + 1, h), a_recv.at[stream, i])
            if i < 5:
                send_rows(stream, i + 1, i + 3, h)

    part = [pl.ds(pl.multiple_of(core * (WIDTH // 2) + k * (WIDTH // 4), WIDTH // 4), WIDTH // 4) for k in (0, 1)]
    away = pl.multiple_of((1 - core) * (WIDTH // 2), WIDTH // 2)
    others = [pl.ds(pl.multiple_of(away + k * (WIDTH // 4), WIDTH // 4), WIDTH // 4) for k in (0, 1)]

    def block(rows, j):
        return wbuf.at[rows, pl.ds(j * COLS, COLS)]

    def send_weights(turn):
        for way in (0, 1):
            rows = part[way ^ turn]
            send(block(rows, 0), block(rows, 1 + way), w_send.at[0], w_recv.at[way, turn], at(dx=1 - 2 * way))

    def pass_weights(turn):
        for way in (0, 1):
            rows = part[way ^ turn]
            held = block(rows, 1 + way)
            wait(held, w_recv.at[way, turn])
            if turn == 0:
                send(held, block(rows, 3), w_send.at[0], w_recv.at[2, way], at(dx=1 - 2 * way))
            send(held, held, w_send.at[1], w_recv.at[3 + way, turn], sibling)

    def pass_last_weights():
        for way in (0, 1):
            held = block(part[way], 3)
            wait(held, w_recv.at[2, way])
            send(held, held, w_send.at[1], w_recv.at[5, way], sibling)

    def take_weights(way):
        for turn in (0, 1):
            k = way ^ turn if way < 2 else turn
            wait(block(others[k], 1 + way), w_recv.at[3 + way, turn])

    send_weights(0)
    send_weights(1)

    def project(first, items, blocks):
        rows = abuf[first : first + items].reshape(items * BLOCK, WIDTH)
        out = dot(rows, wbuf[:, blocks[0] * COLS : (blocks[-1] + 1) * COLS])
        for m in range(items):
            for j in blocks:
                c = CHUNKS.index((first + m, j))
                for h in (0, 1):
                    pbuf[2 * c + h] = out[
                        m * BLOCK + h * HALF : m * BLOCK + (h + 1) * HALF,
                        (j - blocks[0]) * COLS : (j - blocks[0] + 1) * COLS,
                    ]

    up = 1 - 2 * core

    def piece(r, far):
        return pbuf[8 * r + lax.rem(z + far + NZ, NZ)]

    def stage(r, t):
        for side in (0, 1):
            if side > t:
                continue
            way = up if side == 0 else -up
            at_slot, from_slot = 4 * side + t - side, 4 * side + t - side - 1
            total = piece(r, way * (4 - t))
            if t > side:
                wait(rbuf.at[r, from_slot], c_recv.at[r, from_slot])
                total = total + rbuf[r, from_slot].astype(F32)
            sbuf[r, at_slot] = total.astype(BF16)
            send(sbuf.at[r, at_slot], rbuf.at[r, at_slot], c_send.at[0], c_recv.at[r, at_slot], at(dz=way))

    own_half, own_chunk = lax.rem(z, 2), z // 2

    def pick(values):
        out = values[3]
        for k in range(3):
            out = jnp.where(own_chunk == k, values[k], out)
        return out

    def place(r):
        chunks = CHUNKS[4 * r : 4 * r + 4]
        j = pick([c[1] for c in chunks])
        dx = jnp.where(j == 1, NX - 1, jnp.where(j == 0, 0, j - 1))
        steps = pick([(c[0] + 1) // 2 for c in chunks])
        sign = pick([1 if c[0] % 2 == 0 else -1 for c in chunks]) * (1 - 2 * own_half)
        item_y = lax.rem(y + sign * steps + 2 * NY, NY)
        dz = 2 * x + item_y // 4 - z
        row = pl.multiple_of(lax.rem(item_y, 4) * BLOCK + own_half * HALF, HALF)
        return dx, dz, row, (dx == 0) & (dz == 0)

    def finish(r):
        total = piece(r, 0)
        for slot in (3, 6):
            wait(rbuf.at[r, slot], c_recv.at[r, slot])
            total = total + rbuf[r, slot].astype(F32)
        sbuf[r, 7] = total.astype(BF16)
        dx, dz, row, stays = place(r)
        rows = rec_ref.at[pl.ds(row, HALF)]

        @pl.when(stays)
        def _():
            pltpu.make_async_copy(sbuf.at[r, 7], rows, out_recv.at[0]).start()

        @pl.when(jnp.logical_not(stays))
        def _():
            send(sbuf.at[r, 7], rows, f_send.at[r], out_recv.at[0], at(dx=dx, dz=dz))

    def send_context():
        cbuf[x, y] = attend(q_ref, f_ref, c_ref, len_ref)
        for k in range(1, NY):
            send(cbuf.at[x, y], cbuf.at[x, y], d_send.at[0], d_recv.at[0], at(dy=k))

    def pass_context():
        wait(cbuf.at[x, pl.ds(0, NY - 1)], d_recv.at[0])
        for k in range(1, NX):
            send(cbuf.at[x], cbuf.at[x], d_send.at[1], d_recv.at[1], at(dx=k))

    def project_decode():
        wait(cbuf.at[pl.ds(0, NX - 1)], d_recv.at[1])
        for g in range(NX):
            rows = cbuf[g].reshape(NY * 16, 512)
            low = dot(rows, wbuf[0:512, 0:COLS]).reshape(NY, 16, COLS)
            high = dot(rows, wbuf[512:1024, 0:COLS]).reshape(NY, 16, COLS)
            zs[2 * g : 2 * g + 2] = (low[:, :8] + high[:, 8:]).reshape(2, 32, COLS).astype(BF16)
        zr[z] = zs[z]
        for k in range(1, NZ):
            send(zs.at[lax.rem(z + k, NZ)], zr.at[z], d_send.at[2], d_recv.at[2], at(dz=k))

    def hand_over():
        wait(zr.at[pl.ds(0, NZ - 1)], d_recv.at[2])
        total = zr[0].astype(F32)
        for k in range(1, NZ):
            total = total + zr[k].astype(F32)
        decoded = total.astype(BF16)
        dec_ref[...] = decoded
        maps = placement(dest_ref)
        out = dot(maps[0], decoded[:, :128]) + dot(maps[1], decoded[:, 128:])
        h1s[...] = out.astype(BF16).reshape(NY, 16, 128)
        h1r[y] = h1s[y]
        for k in range(1, NY):
            send(h1s.at[lax.rem(y + k, NY)], h1r.at[y], d_send.at[3], d_recv.at[3], at(dy=k))

    def hand_on():
        wait(h1r.at[pl.ds(0, NY - 1)], d_recv.at[3])
        h2s[...] = dot(regroup(), h1r[...].reshape(128, 128)).astype(BF16).reshape(NX, 32, 128)
        h2r[x] = h2s[x]
        for k in range(1, NX):
            send(h2s.at[lax.rem(x + k, NX)], h2r.at[x], d_send.at[4], d_recv.at[4], at(dx=k))

    def take():
        wait(h2r.at[pl.ds(0, NX - 1)], d_recv.at[4])
        hand_ref[...] = dot(regroup_last(), h2r[...].reshape(128, 128)).astype(BF16)

    send_context()
    gather(0)
    pass_weights(0)
    gather(1)
    pass_weights(1)
    project(0, 3, (0,))
    take_weights(0)
    take_weights(1)
    project(0, 3, (1, 2))
    stage(0, 0)
    stage(1, 0)
    pass_context()
    gather(2)
    pass_last_weights()
    project(3, 1, (0, 1, 2))
    take_weights(2)
    project(0, 4, (3,))
    starts = [(0, 1), (2, 3), (4,), (5,), (6, 7)]
    before = {
        2: lambda: (gather(3), project(4, 1, range(NX))),
        3: lambda: (gather(4), project(5, 1, range(NX)), project_decode()),
        4: lambda: (gather(5), project(6, 1, range(NX)), gather(6), project(7, 1, range(NX))),
        5: hand_over,
        6: hand_on,
        7: take,
    }
    for slot in range(1, 9):
        if slot in before:
            before[slot]()
        for t in range(5):
            for r in starts[slot - t] if 0 <= slot - t < len(starts) else ():
                stage(r, t) if t < 4 else finish(r)

    wait(rec_ref, out_recv.at[0])
    for r in range(ROUNDS):
        @pl.when(jnp.logical_not(place(r)[3]))
        def _():
            wait(sbuf.at[r, 7], f_send.at[r])

    wait(sbuf.at[:, pl.ds(0, 7)], c_send.at[0])
    for h in (0, 1):
        wait(abuf.at[pl.ds(0, 7), pl.ds(0, HALF)], a_send.at[h])
    wait(wbuf.at[pl.ds(0, 512), pl.ds(0, 3 * COLS)], w_send.at[0])
    wait(wbuf.at[pl.ds(0, 512), pl.ds(0, 3 * COLS)], w_send.at[1])
    wait(cbuf.at[0, pl.ds(0, NY - 1)], d_send.at[0])
    wait(cbuf.at[pl.ds(0, NX - 1)], d_send.at[1])
    wait(zs.at[pl.ds(0, NZ - 1)], d_send.at[2])
    wait(h1s.at[pl.ds(0, NY - 1)], d_send.at[3])
    wait(h2s.at[pl.ds(0, NX - 1)], d_send.at[4])


def local(query, fresh_key_value, cache, lengths, destination, out_weight, learner_ctx):
    vmem = pl.BlockSpec(memory_space=pltpu.VMEM)
    dma = pltpu.SemaphoreType.DMA
    decoded, handed, recomputed = pl.pallas_call(
        kernel,
        out_shape=(
            jax.ShapeDtypeStruct((32, COLS), BF16),
            jax.ShapeDtypeStruct((128, 128), BF16),
            jax.ShapeDtypeStruct((512, COLS), BF16),
        ),
        in_specs=[pl.BlockSpec(memory_space=pltpu.HBM)] * 7,
        out_specs=(vmem, vmem, vmem),
        scratch_shapes=[
            pltpu.VMEM((8, WIDTH), BF16),
            pltpu.VMEM((16, HEAD_SIZE), BF16),
            pltpu.VMEM((8, 2 * CACHED_POSITIONS, HEAD_SIZE), BF16),
            pltpu.SMEM((8,), jnp.int32),
            pltpu.VMEM((1, 32), jnp.int32),
            pltpu.VMEM((ITEMS, BLOCK, WIDTH), BF16),
            pltpu.VMEM((WIDTH, NX * COLS), BF16),
            pltpu.VMEM((ROUNDS * NZ, HALF, COLS), F32),
            pltpu.VMEM((ROUNDS, NZ - 1, HALF, COLS), BF16),
            pltpu.VMEM((ROUNDS, NZ, HALF, COLS), BF16),
            pltpu.VMEM((NX, NY, 16, 512), BF16),
            pltpu.VMEM((NZ, 32, COLS), BF16),
            pltpu.VMEM((NZ, 32, COLS), BF16),
            pltpu.VMEM((NY, 16, 128), BF16),
            pltpu.VMEM((NY, 16, 128), BF16),
            pltpu.VMEM((NX, 32, 128), BF16),
            pltpu.VMEM((NX, 32, 128), BF16),
            dma((7,)),
            dma((2,)),
            dma((2, 7)),
            dma((2,)),
            dma((6, 2)),
            dma((5,)),
            dma((5,)),
            dma((1,)),
            dma((ROUNDS, NZ - 1)),
            dma((ROUNDS,)),
            dma((1,)),
        ],
        compiler_params=pltpu.CompilerParams(
            collective_id=0, has_side_effects=True, vmem_limit_bytes=63 * 1024 * 1024
        ),
        cost_estimate=pl.CostEstimate(flops=2300000000, bytes_accessed=2500000, transcendentals=33000),
        name="project",
    )(
        query,
        fresh_key_value.reshape(16, HEAD_SIZE),
        cache.reshape(8, 2 * CACHED_POSITIONS, HEAD_SIZE),
        lengths,
        destination.reshape(1, 32),
        out_weight,
        learner_ctx,
    )
    return decoded, handed.reshape(1, 1, 1, 2, 8192), recomputed


def solution(mesh):
    return jax.shard_map(
        local,
        mesh=mesh,
        in_specs=(
            P(("dp", "seq"), "tensor"),
            P(("dp", "seq"), None, "tensor"),
            P(("dp", "seq"), None, None, "tensor"),
            P(("dp", "seq")),
            P(("dp", "tensor"), None),
            P("tensor", "seq"),
            P(("dp", "seq"), "tensor"),
        ),
        out_specs=(
            P(("dp", "tensor"), "seq"),
            P("dp", "seq", "tensor", None, None),
            P(("dp", "tensor"), "seq"),
        ),
        check_vma=False,
    )
```

```python
import functools

import jax
import jax.numpy as jnp
from jax import lax
from jax.experimental import pallas as pl
from jax.experimental.pallas import tpu as pltpu
from jax.sharding import PartitionSpec as P

QUERY_GROUP = 8
HEAD_SIZE = 128
CACHED_POSITIONS = 256
NX, NY, NZ = 4, 8, 8
BLOCK = 128
HALF = 64
WIDTH = 1024
COLS = 256
ITEMS = NY
CHUNKS = [(0, 0), (1, 0), (2, 0), (0, 1), (0, 2), (1, 1), (1, 2), (2, 1), (2, 2), (3, 0), (3, 1), (3, 2)]
CHUNKS += [(m, 3) for m in range(4)] + [(m, j) for m in range(4, ITEMS) for j in range(NX)]
ROUNDS, LATE = 8, 6
MESH_ID = pl.DeviceIdType.MESH
BF16, F32 = jnp.bfloat16, jnp.float32


def dot(a, b):
    return jnp.dot(a, b, preferred_element_type=F32)


def dot_t(a, b):
    return lax.dot_general(a, b, (((1,), (1,)), ((), ())), preferred_element_type=F32)


def iota(shape, dim):
    return lax.broadcasted_iota(jnp.int32, shape, dim)


def one_hot(condition):
    return jnp.where(condition, 1.0, 0.0).astype(BF16)


def attend(q_ref, f_ref, c_ref, len_ref):
    rows = 8
    by_head = jnp.concatenate(
        [q_ref[:, h * HEAD_SIZE : (h + 1) * HEAD_SIZE].astype(F32) for h in range(QUERY_GROUP)], axis=0
    ).astype(BF16)
    r64, c64 = iota((64, 64), 0), iota((64, 64), 1)
    swap = one_hot((r64 % 8) * 8 + r64 // 8 == c64)
    queries = dot(swap, by_head)
    scale = HEAD_SIZE ** (-0.5)
    scores = []
    place = iota((8, 2 * CACHED_POSITIONS), 1)
    for r in range(rows):
        s = dot_t(queries[r * 8 : (r + 1) * 8].astype(BF16), c_ref[r]) * scale
        valid = (place % 2 == 0) & (place < 2 * len_ref[r])
        scores.append(jnp.where(valid, s, -1e30))
    scores = jnp.concatenate(scores, axis=0)
    fresh = f_ref[...]
    fresh_scores = dot_t(queries.astype(BF16), fresh) * scale
    row16, col16 = iota((64, 16), 0), iota((64, 16), 1)
    own = jnp.sum(jnp.where(col16 == 2 * (row16 // 8), fresh_scores, 0.0), axis=1, keepdims=True)
    top = jnp.maximum(jnp.max(scores, axis=1, keepdims=True), own)
    expd = jnp.exp(scores - top)
    own_exp = jnp.exp(own - top)
    total = jnp.sum(expd, axis=1, keepdims=True) + own_exp
    weights = pltpu.roll(expd / total, 1, 1)
    own_weight = jnp.where(col16 == 2 * (row16 // 8) + 1, own_exp / total, 0.0).astype(BF16)
    context = [dot(weights[r * 8 : (r + 1) * 8].astype(BF16), c_ref[r]) for r in range(rows)]
    context = jnp.concatenate(context, axis=0) + dot(own_weight, fresh)
    context = dot(swap, context.astype(BF16))
    halves = [
        jnp.concatenate([context[h * 8 : (h + 1) * 8] for h in range(g * 4, g * 4 + 4)], axis=1) for g in (0, 1)
    ]
    return jnp.concatenate(halves, axis=0).astype(BF16)


def placement(dest_ref):
    dest = dest_ref[...].astype(F32)
    r32, c32 = iota((32, 32), 0), iota((32, 32), 1)
    across = jnp.broadcast_to(dest, (32, 32))
    down = dot(jnp.where(r32 == c32, across, 0.0).astype(BF16), jnp.ones((32, 32), BF16))
    earlier = one_hot((down == across) & (r32 < c32))
    rank = dot(jnp.ones((128, 32), BF16), earlier)
    q, i = iota((128, 32), 0), iota((128, 32), 1)
    target = ((q // 4) % 4) * NY + q // 16
    slot = (q // 2) % 2
    hit = (jnp.broadcast_to(dest, (128, 32)) == target.astype(F32)) & (rank == slot.astype(F32))
    return [one_hot(hit & (q % 2 == h)) for h in (0, 1)]


def regroup():
    r, c = iota((128, 128), 0), iota((128, 128), 1)
    return one_hot((r // 4 % 8) * 16 + (r // 32) * 4 + r % 4 == c)


def regroup_last():
    r, c = iota((128, 128), 0), iota((128, 128), 1)
    return one_hot((r // 2 % 32) * 4 + (r // 64) * 2 + r % 2 == c)


def kernel(
    q_hbm, f_hbm, c_hbm, len_hbm, dest_hbm, w_hbm, a_hbm,
    dec_ref, hand_ref, rec_ref,
    q_ref, f_ref, c_ref, len_ref, dest_ref,
    abuf, wbuf, pbuf, rbuf, sbuf, moved, xs, xr, ls, lr, cbuf, zs, zr, h1s, h1r, h2s, h2r,
    in_sem, a_send, a_recv, w_send, w_recv, d_send, d_recv, c_send, c_recv, m_send, m_recv, f_send, x_send, x_recv, l_send, l_recv, out_recv,
):
    core, seq, z = lax.axis_index("dp"), lax.axis_index("seq"), lax.axis_index("tensor")
    x, y = seq // NY, seq % NY

    def at(dx=0, dy=0, dz=0):
        return {"seq": lax.rem(x + dx + NX, NX) * NY + lax.rem(y + dy + NY, NY), "tensor": lax.rem(z + dz + NZ, NZ)}

    sibling = {"dp": 1 - core}
    partners = (
        [at(dx=k) for k in range(1, NX)] + [at(dy=k) for k in range(1, NY)] + [at(dz=k) for k in range(1, NZ)] + [sibling]
    )

    def send(src, dst, send_sem, recv_sem, device):
        copy = pltpu.make_async_remote_copy(
            src_ref=src, dst_ref=dst, send_sem=send_sem, recv_sem=recv_sem, device_id=device, device_id_type=MESH_ID
        )
        copy.start()

    def wait(ref, sem):
        pltpu.make_async_copy(ref, ref, sem).wait()

    barrier = pltpu.get_barrier_semaphore()
    for device in partners:
        pl.semaphore_signal(barrier, inc=1, device_id=device, device_id_type=MESH_ID)
    loads = [
        pltpu.make_async_copy(src, dst, in_sem.at[k])
        for k, (src, dst) in enumerate(
            [
                (a_hbm, abuf.at[0]), (w_hbm, wbuf.at[:, pl.ds(0, COLS)]), (q_hbm, q_ref), (c_hbm, c_ref),
                (f_hbm, f_ref), (len_hbm, len_ref), (dest_hbm, dest_ref),
            ]
        )
    ]
    for load in loads:
        load.start()
    for load in loads:
        load.wait()
    pl.semaphore_wait(barrier, len(partners))

    def half(item, h):
        return abuf.at[item, pl.ds(pl.multiple_of(h * HALF, HALF), HALF)]

    def send_rows(stream, source, target, h):
        send(half(source, h), half(target, h), a_send.at[stream], a_recv.at[stream, target - 1], at(dy=1 - 2 * stream))

    for i in (0, 1):
        for stream in (0, 1):
            send_rows(stream, 0, i + 1, (i + stream) % 2)

    def gather(i):
        for stream in (0, 1):
            h = (i + stream) % 2
            wait(half(i + 1, h), a_recv.at[stream, i])
            if i < 5:
                send_rows(stream, i + 1, i + 3, h)

    part = [pl.ds(pl.multiple_of(core * (WIDTH // 2) + k * (WIDTH // 4), WIDTH // 4), WIDTH // 4) for k in (0, 1)]
    away = pl.multiple_of((1 - core) * (WIDTH // 2), WIDTH // 2)
    others = [pl.ds(pl.multiple_of(away + k * (WIDTH // 4), WIDTH // 4), WIDTH // 4) for k in (0, 1)]

    def block(rows, j):
        return wbuf.at[rows, pl.ds(j * COLS, COLS)]

    def send_weights(turn):
        for way in (0, 1):
            rows = part[way ^ turn]
            send(block(rows, 0), block(rows, 1 + way), w_send.at[0], w_recv.at[way, turn], at(dx=1 - 2 * way))

    def pass_weights(turn):
        for way in (0, 1):
            rows = part[way ^ turn]
            held = block(rows, 1 + way)
            wait(held, w_recv.at[way, turn])
            if turn == 0:
                send(held, block(rows, 3), w_send.at[0], w_recv.at[2, way], at(dx=1 - 2 * way))
            send(held, held, w_send.at[1], w_recv.at[3 + way, turn], sibling)

    def pass_last_weights():
        for way in (0, 1):
            held = block(part[way], 3)
            wait(held, w_recv.at[2, way])
            send(held, held, w_send.at[1], w_recv.at[5, way], sibling)

    def take_weights(way):
        for turn in (0, 1):
            k = way ^ turn if way < 2 else turn
            wait(block(others[k], 1 + way), w_recv.at[3 + way, turn])

    send_weights(0)
    send_weights(1)

    def project(first, items, blocks):
        rows = abuf[first : first + items].reshape(items * BLOCK, WIDTH)
        out = dot(rows, wbuf[:, blocks[0] * COLS : (blocks[-1] + 1) * COLS])
        for m in range(items):
            for j in blocks:
                c = CHUNKS.index((first + m, j))
                for h in (0, 1):
                    pbuf[2 * c + h] = out[
                        m * BLOCK + h * HALF : m * BLOCK + (h + 1) * HALF,
                        (j - blocks[0]) * COLS : (j - blocks[0] + 1) * COLS,
                    ]

    up = 1 - 2 * core

    def piece(r, far):
        return pbuf[8 * r + lax.rem(z + far + NZ, NZ)]

    def stage(r, t):
        for side in (0, 1):
            if side > t:
                continue
            way = up if side == 0 else -up
            at_slot, from_slot = 4 * side + t - side, 4 * side + t - side - 1
            total = piece(r, way * (4 - t))
            if t > side:
                wait(rbuf.at[r, from_slot], c_recv.at[r, from_slot])
                total = total + rbuf[r, from_slot].astype(F32)
            sbuf[r, at_slot] = total.astype(BF16)
            send(sbuf.at[r, at_slot], rbuf.at[r, at_slot], c_send.at[0], c_recv.at[r, at_slot], at(dz=way))

    own_half, own_chunk = lax.rem(z, 2), z // 2

    def pick(values):
        out = values[3]
        for k in range(3):
            out = jnp.where(own_chunk == k, values[k], out)
        return out

    def spot(m, h):
        steps = (m + 1) // 2
        sign = jnp.where(lax.rem(m + h, 2) == 0, 1, -1)
        return lax.rem(y + sign * steps + 2 * NY, NY)

    def shift(j):
        return jnp.where(j == 1, NX - 1, jnp.where(j == 0, 0, j - 1))

    def out_rows(item_y, h):
        return rec_ref.at[pl.ds(pl.multiple_of(lax.rem(item_y, 4) * BLOCK + h * HALF, HALF), HALF)]

    def keep(src, rows):
        pltpu.make_async_copy(src, rows, out_recv.at[0]).start()

    def finish(r):
        total = piece(r, 0)
        for slot in (3, 6):
            wait(rbuf.at[r, slot], c_recv.at[r, slot])
            total = total + rbuf[r, slot].astype(F32)
        sbuf[r, 7] = total.astype(BF16)
        j = pick([c[1] for c in CHUNKS[4 * r : 4 * r + 4]])

        @pl.when(j == 0)
        def _():
            pltpu.make_async_copy(sbuf.at[r, 7], moved.at[r], m_recv.at[r]).start()

        @pl.when(j > 0)
        def _():
            send(sbuf.at[r, 7], moved.at[r], m_send.at[r], m_recv.at[r], at(dx=shift(j)))

    def home(r):
        chunks = CHUNKS[4 * r : 4 * r + 4]
        item_y = spot(pick([c[0] for c in chunks]), own_half)
        from_x = lax.rem(x - shift(pick([c[1] for c in chunks])) + NX, NX)
        return out_rows(item_y, own_half), 2 * from_x + item_y // 4

    def deliver(r):
        wait(moved.at[r], m_recv.at[r])
        rows, to_z = home(r)

        @pl.when(to_z == z)
        def _():
            keep(moved.at[r], rows)

        @pl.when(to_z != z)
        def _():
            send(moved.at[r], rows, f_send.at[r], out_recv.at[0], at(dz=to_z - z))

    def exchange(r):
        e = r - LATE
        for j in range(NX):
            for h in (0, 1):
                part_sum = pbuf[8 * r + 2 * j + h].astype(BF16)
                if j == 0:
                    xr[e, 0, h] = part_sum
                else:
                    xs[e, j - 1, h] = part_sum
            if j > 0:
                send(xs.at[e, j - 1], xr.at[e, j], x_send.at[e, j - 1], x_recv.at[e, j - 1], at(dx=(0, 3, 1, 2)[j]))

    def exchanged(r):
        for j in range(1, NX):
            wait(xr.at[r - LATE, j], x_recv.at[r - LATE, j - 1])

    def late_messages(r, t, act):
        for side in (0, 1):
            if side > t:
                continue
            way = up if side == 0 else -up
            slot = 4 * side + t - side
            q = lax.rem(z + way * (4 - t) + NZ, NZ)
            for h in (0, 1):
                pl.when(spot(r, h) // 4 == lax.rem(q, 2))(functools.partial(act, r - LATE, t > side, way, slot, q, h))

    def late_piece(e, q, h):
        away = lax.rem(x - q // 2 + NX, NX)
        j = jnp.where(away == 0, 0, jnp.where(away == 3, 1, away + 1))
        return xr[e, j, h].astype(F32)

    def late_send(e, later, way, slot, q, h):
        total = late_piece(e, q, h)
        if later:
            wait(lr.at[e, slot - 1, h], l_recv.at[e, slot - 1, h])
            total = total + lr[e, slot - 1, h].astype(F32)
        ls[e, slot, h] = total.astype(BF16)
        send(ls.at[e, slot, h], lr.at[e, slot, h], l_send.at[e, slot, h], l_recv.at[e, slot, h], at(dz=way))

    def late_drain(e, later, way, slot, q, h):
        wait(ls.at[e, slot, h], l_send.at[e, slot, h])

    def late_finish(r):
        e = r - LATE
        for h in (0, 1):
            item_y = spot(r, h)

            @pl.when(item_y // 4 == lax.rem(z, 2))
            def _():
                total = late_piece(e, z, h)
                for slot in (3, 6):
                    wait(lr.at[e, slot, h], l_recv.at[e, slot, h])
                    total = total + lr[e, slot, h].astype(F32)
                ls[e, 7, h] = total.astype(BF16)
                keep(ls.at[e, 7, h], out_rows(item_y, h))

    def send_context():
        cbuf[x, y] = attend(q_ref, f_ref, c_ref, len_ref)
        for k in range(1, NY):
            send(cbuf.at[x, y], cbuf.at[x, y], d_send.at[0], d_recv.at[0], at(dy=k))

    def pass_context():
        wait(cbuf.at[x, pl.ds(0, NY - 1)], d_recv.at[0])
        for k in range(1, NX):
            send(cbuf.at[x], cbuf.at[x], d_send.at[1], d_recv.at[1], at(dx=k))

    def project_decode():
        wait(cbuf.at[pl.ds(0, NX - 1)], d_recv.at[1])
        for g in range(NX):
            rows = cbuf[g].reshape(NY * 16, 512)
            low = dot(rows, wbuf[0:512, 0:COLS]).reshape(NY, 16, COLS)
            high = dot(rows, wbuf[512:1024, 0:COLS]).reshape(NY, 16, COLS)
            zs[2 * g : 2 * g + 2] = (low[:, :8] + high[:, 8:]).reshape(2, 32, COLS).astype(BF16)
        zr[z] = zs[z]
        for k in range(1, NZ):
            send(zs.at[lax.rem(z + k, NZ)], zr.at[z], d_send.at[2], d_recv.at[2], at(dz=k))

    def hand_over():
        wait(zr.at[pl.ds(0, NZ - 1)], d_recv.at[2])
        total = zr[0].astype(F32)
        for k in range(1, NZ):
            total = total + zr[k].astype(F32)
        decoded = total.astype(BF16)
        dec_ref[...] = decoded
        maps = placement(dest_ref)
        out = dot(maps[0], decoded[:, :128]) + dot(maps[1], decoded[:, 128:])
        h1s[...] = out.astype(BF16).reshape(NY, 16, 128)
        h1r[y] = h1s[y]
        for k in range(1, NY):
            send(h1s.at[lax.rem(y + k, NY)], h1r.at[y], d_send.at[3], d_recv.at[3], at(dy=k))

    def hand_on():
        wait(h1r.at[pl.ds(0, NY - 1)], d_recv.at[3])
        h2s[...] = dot(regroup(), h1r[...].reshape(128, 128)).astype(BF16).reshape(NX, 32, 128)
        h2r[x] = h2s[x]
        for k in range(1, NX):
            send(h2s.at[lax.rem(x + k, NX)], h2r.at[x], d_send.at[4], d_recv.at[4], at(dx=k))

    def take():
        wait(h2r.at[pl.ds(0, NX - 1)], d_recv.at[4])
        hand_ref[...] = dot(regroup_last(), h2r[...].reshape(128, 128)).astype(BF16)

    send_context()
    gather(0)
    pass_weights(0)
    gather(1)
    pass_weights(1)
    project(0, 3, (0,))
    take_weights(0)
    take_weights(1)
    project(0, 3, (1, 2))
    stage(0, 0)
    stage(1, 0)
    pass_context()
    gather(2)
    pass_last_weights()
    project(3, 1, (0, 1, 2))
    take_weights(2)
    project(0, 4, (3,))
    starts = [(0, 1), (2, 3), (4,), (5,)]

    def slot(number):
        for t in range(6):
            for r in starts[number - t] if 0 <= number - t < len(starts) else ():
                stage(r, t) if t < 4 else finish(r) if t == 4 else deliver(r)

    def late(r, t):
        if t == 0:
            exchanged(r)
        late_messages(r, t, late_send) if t < 4 else late_finish(r)

    slot(1)
    gather(3)
    project(4, 1, range(NX))
    slot(2)
    gather(4)
    project(5, 1, range(NX))
    project_decode()
    slot(3)
    gather(5)
    project(6, 1, range(NX))
    exchange(6)
    gather(6)
    project(7, 1, range(NX))
    exchange(7)
    slot(4)
    late(6, 0)
    hand_over()
    late(7, 0)
    late(6, 1)
    slot(5)
    late(7, 1)
    late(6, 2)
    slot(6)
    hand_on()
    late(7, 2)
    late(6, 3)
    slot(7)
    take()
    late(7, 3)
    late(6, 4)
    slot(8)
    late(7, 4)

    wait(rec_ref, out_recv.at[0])
    for r in range(LATE):
        @pl.when(pick([c[1] for c in CHUNKS[4 * r : 4 * r + 4]]) > 0)
        def _():
            wait(sbuf.at[r, 7], m_send.at[r])

        @pl.when(home(r)[1] != z)
        def _():
            wait(moved.at[r], f_send.at[r])

    for r in range(LATE, ROUNDS):
        for t in range(4):
            late_messages(r, t, late_drain)
        for j in range(NX - 1):
            wait(xs.at[r - LATE, j], x_send.at[r - LATE, j])
    wait(sbuf.at[:, pl.ds(0, 7)], c_send.at[0])
    for h in (0, 1):
        wait(abuf.at[pl.ds(0, 7), pl.ds(0, HALF)], a_send.at[h])
    wait(wbuf.at[pl.ds(0, 512), pl.ds(0, 3 * COLS)], w_send.at[0])
    wait(wbuf.at[pl.ds(0, 512), pl.ds(0, 3 * COLS)], w_send.at[1])
    wait(cbuf.at[0, pl.ds(0, NY - 1)], d_send.at[0])
    wait(cbuf.at[pl.ds(0, NX - 1)], d_send.at[1])
    wait(zs.at[pl.ds(0, NZ - 1)], d_send.at[2])
    wait(h1s.at[pl.ds(0, NY - 1)], d_send.at[3])
    wait(h2s.at[pl.ds(0, NX - 1)], d_send.at[4])


def local(query, fresh_key_value, cache, lengths, destination, out_weight, learner_ctx):
    vmem = pl.BlockSpec(memory_space=pltpu.VMEM)
    dma = pltpu.SemaphoreType.DMA
    decoded, handed, recomputed = pl.pallas_call(
        kernel,
        out_shape=(
            jax.ShapeDtypeStruct((32, COLS), BF16),
            jax.ShapeDtypeStruct((128, 128), BF16),
            jax.ShapeDtypeStruct((512, COLS), BF16),
        ),
        in_specs=[pl.BlockSpec(memory_space=pltpu.HBM)] * 7,
        out_specs=(vmem, vmem, vmem),
        scratch_shapes=[
            pltpu.VMEM((8, WIDTH), BF16),
            pltpu.VMEM((16, HEAD_SIZE), BF16),
            pltpu.VMEM((8, 2 * CACHED_POSITIONS, HEAD_SIZE), BF16),
            pltpu.SMEM((8,), jnp.int32),
            pltpu.VMEM((1, 32), jnp.int32),
            pltpu.VMEM((ITEMS, BLOCK, WIDTH), BF16),
            pltpu.VMEM((WIDTH, NX * COLS), BF16),
            pltpu.VMEM((ROUNDS * NZ, HALF, COLS), F32),
            pltpu.VMEM((LATE, NZ - 1, HALF, COLS), BF16),
            pltpu.VMEM((LATE, NZ, HALF, COLS), BF16),
            pltpu.VMEM((LATE, HALF, COLS), BF16),
            pltpu.VMEM((ROUNDS - LATE, NX - 1, 2, HALF, COLS), BF16),
            pltpu.VMEM((ROUNDS - LATE, NX, 2, HALF, COLS), BF16),
            pltpu.VMEM((ROUNDS - LATE, NZ, 2, HALF, COLS), BF16),
            pltpu.VMEM((ROUNDS - LATE, NZ - 1, 2, HALF, COLS), BF16),
            pltpu.VMEM((NX, NY, 16, 512), BF16),
            pltpu.VMEM((NZ, 32, COLS), BF16),
            pltpu.VMEM((NZ, 32, COLS), BF16),
            pltpu.VMEM((NY, 16, 128), BF16),
            pltpu.VMEM((NY, 16, 128), BF16),
            pltpu.VMEM((NX, 32, 128), BF16),
            pltpu.VMEM((NX, 32, 128), BF16),
            dma((7,)),
            dma((2,)),
            dma((2, 7)),
            dma((2,)),
            dma((6, 2)),
            dma((5,)),
            dma((5,)),
            dma((1,)),
            dma((LATE, NZ - 1)),
            dma((LATE,)),
            dma((LATE,)),
            dma((LATE,)),
            dma((ROUNDS - LATE, NX - 1)),
            dma((ROUNDS - LATE, NX - 1)),
            dma((ROUNDS - LATE, NZ - 1, 2)),
            dma((ROUNDS - LATE, NZ - 1, 2)),
            dma((1,)),
        ],
        compiler_params=pltpu.CompilerParams(
            collective_id=0, has_side_effects=True, vmem_limit_bytes=63 * 1024 * 1024
        ),
        cost_estimate=pl.CostEstimate(flops=2300000000, bytes_accessed=2500000, transcendentals=33000),
        name="project",
    )(
        query,
        fresh_key_value.reshape(16, HEAD_SIZE),
        cache.reshape(8, 2 * CACHED_POSITIONS, HEAD_SIZE),
        lengths,
        destination.reshape(1, 32),
        out_weight,
        learner_ctx,
    )
    return decoded, handed.reshape(1, 1, 1, 2, 8192), recomputed


def solution(mesh):
    return jax.shard_map(
        local,
        mesh=mesh,
        in_specs=(
            P(("dp", "seq"), "tensor"),
            P(("dp", "seq"), None, "tensor"),
            P(("dp", "seq"), None, None, "tensor"),
            P(("dp", "seq")),
            P(("dp", "tensor"), None),
            P("tensor", "seq"),
            P(("dp", "seq"), "tensor"),
        ),
        out_specs=(
            P(("dp", "tensor"), "seq"),
            P("dp", "seq", "tensor", None, None),
            P(("dp", "tensor"), "seq"),
        ),
        check_vma=False,
    )
```

```python
import functools

import jax
import jax.numpy as jnp
from jax import lax
from jax.experimental import pallas as pl
from jax.experimental.pallas import tpu as pltpu
from jax.sharding import PartitionSpec as P

QUERY_GROUP = 8
HEAD_SIZE = 128
CACHED_POSITIONS = 256
NX, NY, NZ = 4, 8, 8
BLOCK = 128
HALF = 64
WIDTH = 1024
COLS = 256
ITEMS = NY
CHUNKS = [(0, 0), (1, 0), (2, 0), (0, 1), (0, 2), (1, 1), (1, 2), (2, 1), (2, 2), (3, 0), (3, 1), (3, 2)]
CHUNKS += [(m, 3) for m in range(4)] + [(m, j) for m in range(4, ITEMS) for j in range(NX)]
ROUNDS, LATE = 8, 4
SHORT_HOPS = [
    (0, 0, 4, 1, None), (0, 1, 3, 1, None), (1, 0, 3, 1, 0), (1, 1, 2, 1, 1), (2, 0, 2, 1, 2), (2, 1, 1, 1, 3),
    (3, 0, 1, 1, 4),
]
HOPS = {r: SHORT_HOPS for r in range(LATE, ROUNDS)}

ORDER = [
    ("ctx",), ("g", 0), ("pw", 0), ("g", 1), ("pw", 1), ("pA",), ("tw", 0), ("tw", 1), ("pB",), ("s", 0, 0),
    ("s", 1, 0), ("pctx",), ("g", 2), ("plw",), ("pC",), ("tw", 2), ("pD",), ("s", 2, 0), ("s", 3, 0), ("s", 0, 1),
    ("s", 1, 1), ("g", 3), ("p", 4), ("x", 4), ("s", 2, 1), ("s", 3, 1), ("s", 0, 2), ("s", 1, 2), ("g", 4), ("p", 5),
    ("x", 5), ("e", 4), ("l", 4, 0), ("pd",), ("s", 2, 2), ("s", 3, 2), ("s", 0, 3), ("s", 1, 3), ("g", 5), ("p", 6),
    ("x", 6), ("e", 5), ("l", 5, 0), ("l", 4, 1), ("g", 6), ("p", 7), ("x", 7), ("s", 2, 3), ("s", 3, 3), ("e", 6),
    ("l", 6, 0), ("f", 0), ("f", 1), ("l", 5, 1), ("l", 4, 2), ("e", 7), ("l", 7, 0), ("l", 6, 1), ("ho",), ("f", 2),
    ("f", 3), ("d", 0), ("d", 1), ("l", 5, 2), ("l", 4, 3), ("l", 7, 1), ("l", 6, 2), ("l", 5, 3), ("hon",), ("F", 4),
    ("l", 7, 2), ("l", 6, 3), ("d", 2), ("d", 3), ("F", 5), ("l", 7, 3), ("F", 6), ("take",), ("F", 7),
]
MESH_ID = pl.DeviceIdType.MESH
BF16, F32 = jnp.bfloat16, jnp.float32


def dot(a, b):
    return jnp.dot(a, b, preferred_element_type=F32)


def dot_t(a, b):
    return lax.dot_general(a, b, (((1,), (1,)), ((), ())), preferred_element_type=F32)


def iota(shape, dim):
    return lax.broadcasted_iota(jnp.int32, shape, dim)


def one_hot(condition):
    return jnp.where(condition, 1.0, 0.0).astype(BF16)


def attend(q_ref, f_ref, c_ref, len_ref):
    rows = 8
    by_head = jnp.concatenate(
        [q_ref[:, h * HEAD_SIZE : (h + 1) * HEAD_SIZE].astype(F32) for h in range(QUERY_GROUP)], axis=0
    ).astype(BF16)
    r64, c64 = iota((64, 64), 0), iota((64, 64), 1)
    swap = one_hot((r64 % 8) * 8 + r64 // 8 == c64)
    queries = dot(swap, by_head)
    scale = HEAD_SIZE ** (-0.5)
    scores = []
    place = iota((8, 2 * CACHED_POSITIONS), 1)
    for r in range(rows):
        s = dot_t(queries[r * 8 : (r + 1) * 8].astype(BF16), c_ref[r]) * scale
        valid = (place % 2 == 0) & (place < 2 * len_ref[r])
        scores.append(jnp.where(valid, s, -1e30))
    scores = jnp.concatenate(scores, axis=0)
    fresh = f_ref[...]
    fresh_scores = dot_t(queries.astype(BF16), fresh) * scale
    row16, col16 = iota((64, 16), 0), iota((64, 16), 1)
    own = jnp.sum(jnp.where(col16 == 2 * (row16 // 8), fresh_scores, 0.0), axis=1, keepdims=True)
    top = jnp.maximum(jnp.max(scores, axis=1, keepdims=True), own)
    expd = jnp.exp(scores - top)
    own_exp = jnp.exp(own - top)
    total = jnp.sum(expd, axis=1, keepdims=True) + own_exp
    weights = pltpu.roll(expd / total, 1, 1)
    own_weight = jnp.where(col16 == 2 * (row16 // 8) + 1, own_exp / total, 0.0).astype(BF16)
    context = [dot(weights[r * 8 : (r + 1) * 8].astype(BF16), c_ref[r]) for r in range(rows)]
    context = jnp.concatenate(context, axis=0) + dot(own_weight, fresh)
    context = dot(swap, context.astype(BF16))
    halves = [
        jnp.concatenate([context[h * 8 : (h + 1) * 8] for h in range(g * 4, g * 4 + 4)], axis=1) for g in (0, 1)
    ]
    return jnp.concatenate(halves, axis=0).astype(BF16)


def placement(dest_ref):
    dest = dest_ref[...].astype(F32)
    r32, c32 = iota((32, 32), 0), iota((32, 32), 1)
    across = jnp.broadcast_to(dest, (32, 32))
    down = dot(jnp.where(r32 == c32, across, 0.0).astype(BF16), jnp.ones((32, 32), BF16))
    earlier = one_hot((down == across) & (r32 < c32))
    rank = dot(jnp.ones((128, 32), BF16), earlier)
    q, i = iota((128, 32), 0), iota((128, 32), 1)
    target = ((q // 4) % 4) * NY + q // 16
    slot = (q // 2) % 2
    hit = (jnp.broadcast_to(dest, (128, 32)) == target.astype(F32)) & (rank == slot.astype(F32))
    return [one_hot(hit & (q % 2 == h)) for h in (0, 1)]


def regroup():
    r, c = iota((128, 128), 0), iota((128, 128), 1)
    return one_hot((r // 4 % 8) * 16 + (r // 32) * 4 + r % 4 == c)


def regroup_last():
    r, c = iota((128, 128), 0), iota((128, 128), 1)
    return one_hot((r // 4) * 4 + (r % 2) * 2 + r // 2 % 2 == c)


def kernel(
    q_hbm, f_hbm, c_hbm, len_hbm, dest_hbm, w_hbm, a_hbm,
    dec_ref, hand_ref, rec_ref,
    q_ref, f_ref, c_ref, len_ref, dest_ref,
    abuf, wbuf, pbuf, rbuf, sbuf, moved, xs, xr, ls, lr, cbuf, zs, zr, h1s, h1r, h2s, h2r,
    in_sem, a_send, a_recv, w_send, w_recv, d_send, d_recv, c_send, c_recv, m_send, m_recv, f_send, x_send, x_recv, l_send, l_recv, out_recv,
):
    core, seq, z = lax.axis_index("dp"), lax.axis_index("seq"), lax.axis_index("tensor")
    x, y = seq // NY, seq % NY

    def at(dx=0, dy=0, dz=0):
        return {"seq": lax.rem(x + dx + NX, NX) * NY + lax.rem(y + dy + NY, NY), "tensor": lax.rem(z + dz + NZ, NZ)}

    sibling = {"dp": 1 - core}
    partners = (
        [at(dx=k) for k in range(1, NX)] + [at(dy=k) for k in range(1, NY)] + [at(dz=k) for k in range(1, NZ)] + [sibling]
    )

    def send(src, dst, send_sem, recv_sem, device):
        copy = pltpu.make_async_remote_copy(
            src_ref=src, dst_ref=dst, send_sem=send_sem, recv_sem=recv_sem, device_id=device, device_id_type=MESH_ID
        )
        copy.start()

    def wait(ref, sem):
        pltpu.make_async_copy(ref, ref, sem).wait()

    barrier = pltpu.get_barrier_semaphore()
    for device in partners:
        pl.semaphore_signal(barrier, inc=1, device_id=device, device_id_type=MESH_ID)
    loads = [
        pltpu.make_async_copy(src, dst, in_sem.at[k])
        for k, (src, dst) in enumerate(
            [
                (a_hbm, abuf.at[0]), (w_hbm, wbuf.at[:, pl.ds(0, COLS)]), (q_hbm, q_ref), (c_hbm, c_ref),
                (f_hbm, f_ref), (len_hbm, len_ref), (dest_hbm, dest_ref),
            ]
        )
    ]
    for load in loads:
        load.start()
    for load in loads:
        load.wait()
    pl.semaphore_wait(barrier, len(partners))

    def half(item, h):
        return abuf.at[item, pl.ds(pl.multiple_of(h * HALF, HALF), HALF)]

    def send_rows(stream, source, target, h):
        send(half(source, h), half(target, h), a_send.at[stream], a_recv.at[stream, target - 1], at(dy=1 - 2 * stream))

    for i in (0, 1):
        for stream in (0, 1):
            send_rows(stream, 0, i + 1, (i + stream) % 2)

    def gather(i):
        for stream in (0, 1):
            h = (i + stream) % 2
            wait(half(i + 1, h), a_recv.at[stream, i])
            if i < 5:
                send_rows(stream, i + 1, i + 3, h)

    part = [pl.ds(pl.multiple_of(core * (WIDTH // 2) + k * (WIDTH // 4), WIDTH // 4), WIDTH // 4) for k in (0, 1)]
    away = pl.multiple_of((1 - core) * (WIDTH // 2), WIDTH // 2)
    others = [pl.ds(pl.multiple_of(away + k * (WIDTH // 4), WIDTH // 4), WIDTH // 4) for k in (0, 1)]

    def block(rows, j):
        return wbuf.at[rows, pl.ds(j * COLS, COLS)]

    def send_weights(turn):
        for way in (0, 1):
            rows = part[way ^ turn]
            send(block(rows, 0), block(rows, 1 + way), w_send.at[0], w_recv.at[way, turn], at(dx=1 - 2 * way))

    def pass_weights(turn):
        for way in (0, 1):
            rows = part[way ^ turn]
            held = block(rows, 1 + way)
            wait(held, w_recv.at[way, turn])
            if turn == 0:
                send(held, block(rows, 3), w_send.at[0], w_recv.at[2, way], at(dx=1 - 2 * way))
            send(held, held, w_send.at[1], w_recv.at[3 + way, turn], sibling)

    def pass_last_weights():
        for way in (0, 1):
            held = block(part[way], 3)
            wait(held, w_recv.at[2, way])
            send(held, held, w_send.at[1], w_recv.at[5, way], sibling)

    def take_weights(way):
        for turn in (0, 1):
            k = way ^ turn if way < 2 else turn
            wait(block(others[k], 1 + way), w_recv.at[3 + way, turn])

    send_weights(0)
    send_weights(1)

    def project(first, items, blocks):
        rows = abuf[first : first + items].reshape(items * BLOCK, WIDTH)
        out = dot(rows, wbuf[:, blocks[0] * COLS : (blocks[-1] + 1) * COLS])
        for m in range(items):
            for j in blocks:
                c = CHUNKS.index((first + m, j))
                for h in (0, 1):
                    pbuf[2 * c + h] = out[
                        m * BLOCK + h * HALF : m * BLOCK + (h + 1) * HALF,
                        (j - blocks[0]) * COLS : (j - blocks[0] + 1) * COLS,
                    ]

    up = 1 - 2 * core

    def piece(r, far):
        return pbuf[8 * r + lax.rem(z + far + NZ, NZ)]

    def stage(r, t):
        for side in (0, 1):
            if side > t:
                continue
            way = up if side == 0 else -up
            at_slot, from_slot = 4 * side + t - side, 4 * side + t - side - 1
            total = piece(r, way * (4 - t))
            if t > side:
                wait(rbuf.at[r, from_slot], c_recv.at[r, from_slot])
                total = total + rbuf[r, from_slot].astype(F32)
            sbuf[r, at_slot] = total.astype(BF16)
            send(sbuf.at[r, at_slot], rbuf.at[r, at_slot], c_send.at[0], c_recv.at[r, at_slot], at(dz=way))

    own_half, own_chunk = lax.rem(z, 2), z // 2

    def pick(values):
        out = values[3]
        for k in range(3):
            out = jnp.where(own_chunk == k, values[k], out)
        return out

    def spot(m, h):
        steps = (m + 1) // 2
        sign = jnp.where(lax.rem(m + h, 2) == 0, 1, -1)
        return lax.rem(y + sign * steps + 2 * NY, NY)

    def shift(j):
        return jnp.where(j == 1, NX - 1, jnp.where(j == 0, 0, j - 1))

    def out_rows(item_y, h):
        return rec_ref.at[pl.ds(pl.multiple_of(lax.rem(item_y, 4) * BLOCK + h * HALF, HALF), HALF)]

    def keep(src, rows):
        pltpu.make_async_copy(src, rows, out_recv.at[0]).start()

    def finish(r):
        total = piece(r, 0)
        for slot in (3, 6):
            wait(rbuf.at[r, slot], c_recv.at[r, slot])
            total = total + rbuf[r, slot].astype(F32)
        sbuf[r, 7] = total.astype(BF16)
        j = pick([c[1] for c in CHUNKS[4 * r : 4 * r + 4]])

        @pl.when(j == 0)
        def _():
            pltpu.make_async_copy(sbuf.at[r, 7], moved.at[r], m_recv.at[r]).start()

        @pl.when(j > 0)
        def _():
            send(sbuf.at[r, 7], moved.at[r], m_send.at[r], m_recv.at[r], at(dx=shift(j)))

    def home(r):
        chunks = CHUNKS[4 * r : 4 * r + 4]
        item_y = spot(pick([c[0] for c in chunks]), own_half)
        from_x = lax.rem(x - shift(pick([c[1] for c in chunks])) + NX, NX)
        return out_rows(item_y, own_half), 2 * from_x + item_y // 4

    def deliver(r):
        wait(moved.at[r], m_recv.at[r])
        rows, to_z = home(r)

        @pl.when(to_z == z)
        def _():
            keep(moved.at[r], rows)

        @pl.when(to_z != z)
        def _():
            send(moved.at[r], rows, f_send.at[r], out_recv.at[0], at(dz=to_z - z))

    def exchange(r):
        e = r - LATE
        for j in range(NX):
            for h in (0, 1):
                part_sum = pbuf[8 * r + 2 * j + h].astype(BF16)
                if j == 0:
                    xr[e, 0, h] = part_sum
                else:
                    xs[e, j - 1, h] = part_sum
            if j > 0:
                send(xs.at[e, j - 1], xr.at[e, j], x_send.at[e, j - 1], x_recv.at[e, j - 1], at(dx=(0, 3, 1, 2)[j]))

    def exchanged(r):
        for j in range(1, NX):
            wait(xr.at[r - LATE, j], x_recv.at[r - LATE, j - 1])

    def late_messages(r, t, act):
        for k, (turn, side, far, hop, after) in enumerate(HOPS[r]):
            if turn == t:
                way = up if side == 0 else -up
                q = lax.rem(z + way * far + NZ, NZ)
                for h in (0, 1):
                    pl.when(spot(r, h) // 4 == lax.rem(q, 2))(
                        functools.partial(act, r - LATE, k, after, way * hop, q, h)
                    )

    def late_piece(e, q, h):
        away = lax.rem(x - q // 2 + NX, NX)
        j = jnp.where(away == 0, 0, jnp.where(away == 3, 1, away + 1))
        return xr[e, j, h].astype(F32)

    def late_send(e, k, after, dz, q, h):
        total = late_piece(e, q, h)
        if after is not None:
            wait(lr.at[e, after, h], l_recv.at[e, after, h])
            total = total + lr[e, after, h].astype(F32)
        ls[e, k, h] = total.astype(BF16)
        send(ls.at[e, k, h], lr.at[e, k, h], l_send.at[e, k, h], l_recv.at[e, k, h], at(dz=dz))

    def late_drain(e, k, after, dz, q, h):
        wait(ls.at[e, k, h], l_send.at[e, k, h])

    def late_finish(r):
        e = r - LATE
        ends = [k for k in range(NZ - 1) if k not in [hop[4] for hop in HOPS[r]]]
        for h in (0, 1):
            item_y = spot(r, h)

            @pl.when(item_y // 4 == lax.rem(z, 2))
            def _():
                total = late_piece(e, z, h)
                for k in ends:
                    wait(lr.at[e, k, h], l_recv.at[e, k, h])
                    total = total + lr[e, k, h].astype(F32)
                ls[e, 7, h] = total.astype(BF16)
                keep(ls.at[e, 7, h], out_rows(item_y, h))

    def send_context():
        cbuf[x, y] = attend(q_ref, f_ref, c_ref, len_ref)
        for k in range(1, NY):
            send(cbuf.at[x, y], cbuf.at[x, y], d_send.at[0], d_recv.at[0], at(dy=k))

    def pass_context():
        wait(cbuf.at[x, pl.ds(0, NY - 1)], d_recv.at[0])
        for k in range(1, NX):
            send(cbuf.at[x], cbuf.at[x], d_send.at[1], d_recv.at[1], at(dx=k))

    def project_decode():
        wait(cbuf.at[pl.ds(0, NX - 1)], d_recv.at[1])
        for g in range(NX):
            rows = cbuf[g].reshape(NY * 16, 512)
            low = dot(rows, wbuf[0:512, 0:COLS]).reshape(NY, 16, COLS)
            high = dot(rows, wbuf[512:1024, 0:COLS]).reshape(NY, 16, COLS)
            zs[2 * g : 2 * g + 2] = (low[:, :8] + high[:, 8:]).reshape(2, 32, COLS).astype(BF16)
        zr[z] = zs[z]
        for k in range(1, NZ):
            send(zs.at[lax.rem(z + k, NZ)], zr.at[z], d_send.at[2], d_recv.at[2], at(dz=k))

    def hand_over():
        wait(zr.at[pl.ds(0, NZ - 1)], d_recv.at[2])
        total = zr[0].astype(F32)
        for k in range(1, NZ):
            total = total + zr[k].astype(F32)
        decoded = total.astype(BF16)
        dec_ref[...] = decoded
        maps = placement(dest_ref)
        out = dot(maps[0], decoded[:, :128]) + dot(maps[1], decoded[:, 128:])
        h1s[...] = out.astype(BF16).reshape(NY, 16, 128)
        h1r[y] = h1s[y]
        for k in range(1, NY):
            send(h1s.at[lax.rem(y + k, NY)], h1r.at[y], d_send.at[3], d_recv.at[3], at(dy=k))

    def hand_on():
        wait(h1r.at[pl.ds(0, NY - 1)], d_recv.at[3])
        h2s[...] = dot(regroup(), h1r[...].reshape(128, 128)).astype(BF16).reshape(NX, 32, 128)
        h2r[x] = h2s[x]
        for k in range(1, NX):
            send(h2s.at[lax.rem(x + k, NX)], h2r.at[x], d_send.at[4], d_recv.at[4], at(dx=k))

    def take():
        wait(h2r.at[pl.ds(0, NX - 1)], d_recv.at[4])
        out = dot(regroup_last(), h2r[...].reshape(128, 128))
        hand_ref[0, 0, 0] = jnp.concatenate([out[2 * k : 2 * k + 2] for k in range(64)], axis=1).astype(BF16)

    tasks = {
        "ctx": send_context, "pctx": pass_context, "pd": project_decode, "ho": hand_over, "hon": hand_on, "take": take,
        "g": gather, "pw": pass_weights, "plw": pass_last_weights, "tw": take_weights,
        "pA": lambda: project(0, 3, (0,)), "pB": lambda: project(0, 3, (1, 2)), "pC": lambda: project(3, 1, (0, 1, 2)),
        "pD": lambda: project(0, 4, (3,)), "p": lambda m: project(m, 1, range(NX)),
        "x": exchange, "e": exchanged, "s": stage, "f": finish, "d": deliver,
        "l": lambda r, t: late_messages(r, t, late_send), "F": late_finish,
    }
    for name, *numbers in ORDER:
        tasks[name](*numbers)

    wait(rec_ref, out_recv.at[0])
    for r in range(LATE):
        @pl.when(pick([c[1] for c in CHUNKS[4 * r : 4 * r + 4]]) > 0)
        def _():
            wait(sbuf.at[r, 7], m_send.at[r])

        @pl.when(home(r)[1] != z)
        def _():
            wait(moved.at[r], f_send.at[r])

    for r in range(LATE, ROUNDS):
        for t in range(4):
            late_messages(r, t, late_drain)
        for j in range(NX - 1):
            wait(xs.at[r - LATE, j], x_send.at[r - LATE, j])
    wait(sbuf.at[:, pl.ds(0, 7)], c_send.at[0])
    for h in (0, 1):
        wait(abuf.at[pl.ds(0, 7), pl.ds(0, HALF)], a_send.at[h])
    wait(wbuf.at[pl.ds(0, 512), pl.ds(0, 3 * COLS)], w_send.at[0])
    wait(wbuf.at[pl.ds(0, 512), pl.ds(0, 3 * COLS)], w_send.at[1])
    wait(cbuf.at[0, pl.ds(0, NY - 1)], d_send.at[0])
    wait(cbuf.at[pl.ds(0, NX - 1)], d_send.at[1])
    wait(zs.at[pl.ds(0, NZ - 1)], d_send.at[2])
    wait(h1s.at[pl.ds(0, NY - 1)], d_send.at[3])
    wait(h2s.at[pl.ds(0, NX - 1)], d_send.at[4])


def emit(*refs):
    given, out, held, sems = refs[:3], refs[3:6], refs[6:9], refs[9]
    loads = [pltpu.make_async_copy(given[k], held[k], sems.at[0, k]) for k in range(3)]
    stores = [pltpu.make_async_copy(held[k], out[k], sems.at[1, k]) for k in range(3)]
    for load in loads:
        load.start()
    for load, store in zip(loads, stores):
        load.wait()
        store.start()
    for store in stores:
        store.wait()


def local(query, fresh_key_value, cache, lengths, destination, out_weight, learner_ctx):
    vmem = pl.BlockSpec(memory_space=pltpu.VMEM)
    dma = pltpu.SemaphoreType.DMA
    results = pl.pallas_call(
        kernel,
        out_shape=(
            jax.ShapeDtypeStruct((32, COLS), BF16),
            jax.ShapeDtypeStruct((1, 1, 1, 2, 8192), BF16),
            jax.ShapeDtypeStruct((512, COLS), BF16),
        ),
        in_specs=[pl.BlockSpec(memory_space=pltpu.HBM)] * 7,
        out_specs=(vmem, vmem, vmem),
        scratch_shapes=[
            pltpu.VMEM((8, WIDTH), BF16),
            pltpu.VMEM((16, HEAD_SIZE), BF16),
            pltpu.VMEM((8, 2 * CACHED_POSITIONS, HEAD_SIZE), BF16),
            pltpu.SMEM((8,), jnp.int32),
            pltpu.VMEM((1, 32), jnp.int32),
            pltpu.VMEM((ITEMS, BLOCK, WIDTH), BF16),
            pltpu.VMEM((WIDTH, NX * COLS), BF16),
            pltpu.VMEM((ROUNDS * NZ, HALF, COLS), F32),
            pltpu.VMEM((LATE, NZ - 1, HALF, COLS), BF16),
            pltpu.VMEM((LATE, NZ, HALF, COLS), BF16),
            pltpu.VMEM((LATE, HALF, COLS), BF16),
            pltpu.VMEM((ROUNDS - LATE, NX - 1, 2, HALF, COLS), BF16),
            pltpu.VMEM((ROUNDS - LATE, NX, 2, HALF, COLS), BF16),
            pltpu.VMEM((ROUNDS - LATE, NZ, 2, HALF, COLS), BF16),
            pltpu.VMEM((ROUNDS - LATE, NZ - 1, 2, HALF, COLS), BF16),
            pltpu.VMEM((NX, NY, 16, 512), BF16),
            pltpu.VMEM((NZ, 32, COLS), BF16),
            pltpu.VMEM((NZ, 32, COLS), BF16),
            pltpu.VMEM((NY, 16, 128), BF16),
            pltpu.VMEM((NY, 16, 128), BF16),
            pltpu.VMEM((NX, 32, 128), BF16),
            pltpu.VMEM((NX, 32, 128), BF16),
            dma((7,)),
            dma((2,)),
            dma((2, 7)),
            dma((2,)),
            dma((6, 2)),
            dma((5,)),
            dma((5,)),
            dma((1,)),
            dma((LATE, NZ - 1)),
            dma((LATE,)),
            dma((LATE,)),
            dma((LATE,)),
            dma((ROUNDS - LATE, NX - 1)),
            dma((ROUNDS - LATE, NX - 1)),
            dma((ROUNDS - LATE, NZ - 1, 2)),
            dma((ROUNDS - LATE, NZ - 1, 2)),
            dma((1,)),
        ],
        compiler_params=pltpu.CompilerParams(
            collective_id=0, has_side_effects=True, vmem_limit_bytes=63 * 1024 * 1024
        ),
        cost_estimate=pl.CostEstimate(flops=2300000000, bytes_accessed=2500000, transcendentals=33000),
        name="project",
    )(
        query,
        fresh_key_value.reshape(16, HEAD_SIZE),
        cache.reshape(8, 2 * CACHED_POSITIONS, HEAD_SIZE),
        lengths,
        destination.reshape(1, 32),
        out_weight,
        learner_ctx,
    )
    in_hbm = pl.BlockSpec(memory_space=pltpu.HBM)
    return pl.pallas_call(
        emit,
        out_shape=tuple(jax.ShapeDtypeStruct(r.shape, r.dtype) for r in results),
        in_specs=[in_hbm] * 3,
        out_specs=(in_hbm,) * 3,
        scratch_shapes=[pltpu.VMEM(r.shape, r.dtype) for r in results] + [dma((2, 3))],
        compiler_params=pltpu.CompilerParams(vmem_limit_bytes=63 * 1024 * 1024),
        name="emit",
    )(*results)


def solution(mesh):
    return jax.shard_map(
        local,
        mesh=mesh,
        in_specs=(
            P(("dp", "seq"), "tensor"),
            P(("dp", "seq"), None, "tensor"),
            P(("dp", "seq"), None, None, "tensor"),
            P(("dp", "seq")),
            P(("dp", "tensor"), None),
            P("tensor", "seq"),
            P(("dp", "seq"), "tensor"),
        ),
        out_specs=(
            P(("dp", "tensor"), "seq"),
            P("dp", "seq", "tensor", None, None),
            P(("dp", "tensor"), "seq"),
        ),
        check_vma=False,
    )
```

```python
import functools

import jax
import jax.numpy as jnp
from jax import lax
from jax.experimental import pallas as pl
from jax.experimental.pallas import tpu as pltpu
from jax.sharding import PartitionSpec as P

QUERY_GROUP = 8
HEAD_SIZE = 128
CACHED_POSITIONS = 256
NX, NY, NZ = 4, 8, 8
BLOCK = 128
HALF = 64
WIDTH = 1024
COLS = 256
ITEMS = NY
CHUNKS = [(0, 0), (1, 0), (2, 0), (0, 1), (0, 2), (1, 1), (1, 2), (2, 1), (2, 2), (3, 0), (3, 1), (3, 2)]
CHUNKS += [(m, 3) for m in range(4)] + [(m, j) for m in range(4, ITEMS) for j in range(NX)]
ROUNDS, LATE = 8, 4
SHORT_HOPS = [
    (0, 0, 4, 1, None), (0, 1, 3, 1, None), (1, 0, 3, 1, 0), (1, 1, 2, 1, 1), (2, 0, 2, 1, 2), (2, 1, 1, 1, 3),
    (3, 0, 1, 1, 4),
]
HOPS = {r: SHORT_HOPS for r in range(LATE, ROUNDS)}

ORDER = [
    ("ctx",), ("g", 0), ("pw", 0), ("g", 1), ("pw", 1), ("pA",), ("tw", 0), ("tw", 1), ("pB",), ("s", 0, 0),
    ("s", 1, 0), ("g", 2), ("plw",), ("pC",), ("tw", 2), ("pD",), ("s", 2, 0), ("s", 3, 0), ("s", 0, 1), ("s", 1, 1),
    ("g", 3), ("cs",), ("p", 4), ("x", 4), ("s", 2, 1), ("s", 3, 1), ("s", 0, 2), ("s", 1, 2), ("g", 4), ("p", 5),
    ("x", 5), ("e", 4), ("l", 4, 0), ("s", 2, 2), ("s", 3, 2), ("s", 0, 3), ("s", 1, 3), ("g", 5), ("p", 6), ("x", 6),
    ("e", 5), ("l", 5, 0), ("l", 4, 1), ("pd",), ("g", 6), ("p", 7), ("x", 7), ("s", 2, 3), ("s", 3, 3), ("e", 6),
    ("l", 6, 0), ("sd",), ("f", 0), ("f", 1), ("l", 5, 1), ("l", 4, 2), ("e", 7), ("l", 7, 0), ("l", 6, 1), ("ho",),
    ("f", 2), ("f", 3), ("d", 0), ("d", 1), ("l", 5, 2), ("l", 4, 3), ("l", 7, 1), ("l", 6, 2), ("l", 5, 3), ("hon",),
    ("F", 4), ("l", 7, 2), ("l", 6, 3), ("d", 2), ("d", 3), ("F", 5), ("l", 7, 3), ("F", 6), ("take",), ("F", 7),
]
MESH_ID = pl.DeviceIdType.MESH
BF16, F32 = jnp.bfloat16, jnp.float32


def dot(a, b):
    return jnp.dot(a, b, preferred_element_type=F32)


def dot_t(a, b):
    return lax.dot_general(a, b, (((1,), (1,)), ((), ())), preferred_element_type=F32)


def iota(shape, dim):
    return lax.broadcasted_iota(jnp.int32, shape, dim)


def one_hot(condition):
    return jnp.where(condition, 1.0, 0.0).astype(BF16)


def attend(q_ref, f_ref, c_ref, len_ref):
    rows = 8
    by_head = jnp.concatenate(
        [q_ref[:, h * HEAD_SIZE : (h + 1) * HEAD_SIZE].astype(F32) for h in range(QUERY_GROUP)], axis=0
    ).astype(BF16)
    r64, c64 = iota((64, 64), 0), iota((64, 64), 1)
    swap = one_hot((r64 % 8) * 8 + r64 // 8 == c64)
    queries = dot(swap, by_head)
    scale = HEAD_SIZE ** (-0.5)
    scores = []
    place = iota((8, 2 * CACHED_POSITIONS), 1)
    for r in range(rows):
        s = dot_t(queries[r * 8 : (r + 1) * 8].astype(BF16), c_ref[r]) * scale
        valid = (place % 2 == 0) & (place < 2 * len_ref[r])
        scores.append(jnp.where(valid, s, -1e30))
    scores = jnp.concatenate(scores, axis=0)
    fresh = f_ref[...]
    fresh_scores = dot_t(queries.astype(BF16), fresh) * scale
    row16, col16 = iota((64, 16), 0), iota((64, 16), 1)
    own = jnp.sum(jnp.where(col16 == 2 * (row16 // 8), fresh_scores, 0.0), axis=1, keepdims=True)
    top = jnp.maximum(jnp.max(scores, axis=1, keepdims=True), own)
    expd = jnp.exp(scores - top)
    own_exp = jnp.exp(own - top)
    total = jnp.sum(expd, axis=1, keepdims=True) + own_exp
    weights = pltpu.roll(expd / total, 1, 1)
    own_weight = jnp.where(col16 == 2 * (row16 // 8) + 1, own_exp / total, 0.0).astype(BF16)
    context = [dot(weights[r * 8 : (r + 1) * 8].astype(BF16), c_ref[r]) for r in range(rows)]
    context = jnp.concatenate(context, axis=0) + dot(own_weight, fresh)
    context = dot(swap, context.astype(BF16))
    halves = [
        jnp.concatenate([context[h * 8 : (h + 1) * 8] for h in range(g * 4, g * 4 + 4)], axis=1) for g in (0, 1)
    ]
    return jnp.concatenate(halves, axis=0).astype(BF16)


def placement(dest_ref):
    dest = dest_ref[...].astype(F32)
    r32, c32 = iota((32, 32), 0), iota((32, 32), 1)
    across = jnp.broadcast_to(dest, (32, 32))
    down = dot(jnp.where(r32 == c32, across, 0.0).astype(BF16), jnp.ones((32, 32), BF16))
    earlier = one_hot((down == across) & (r32 < c32))
    rank = dot(jnp.ones((128, 32), BF16), earlier)
    q, i = iota((128, 32), 0), iota((128, 32), 1)
    target = ((q // 4) % 4) * NY + q // 16
    slot = (q // 2) % 2
    hit = (jnp.broadcast_to(dest, (128, 32)) == target.astype(F32)) & (rank == slot.astype(F32))
    return [one_hot(hit & (q % 2 == h)) for h in (0, 1)]


def regroup():
    r, c = iota((128, 128), 0), iota((128, 128), 1)
    return one_hot((r // 4 % 8) * 16 + (r // 32) * 4 + r % 4 == c)


def regroup_last():
    r, c = iota((128, 128), 0), iota((128, 128), 1)
    return one_hot((r // 4) * 4 + (r % 2) * 2 + r // 2 % 2 == c)


def kernel(
    q_hbm, f_hbm, c_hbm, len_hbm, dest_hbm, w_hbm, a_hbm,
    dec_ref, hand_ref, rec_ref,
    q_ref, f_ref, c_ref, len_ref, dest_ref,
    abuf, wbuf, pbuf, rbuf, sbuf, moved, xs, xr, ls, lr, cbuf, xd, zs, zr, h1s, h1r, h2s, h2r,
    in_sem, a_send, a_recv, w_send, w_recv, d_send, d_recv, c_send, c_recv, m_send, m_recv, f_send, x_send, x_recv, l_send, l_recv, out_recv,
):
    core, seq, z = lax.axis_index("dp"), lax.axis_index("seq"), lax.axis_index("tensor")
    x, y = seq // NY, seq % NY

    def at(dx=0, dy=0, dz=0):
        return {"seq": lax.rem(x + dx + NX, NX) * NY + lax.rem(y + dy + NY, NY), "tensor": lax.rem(z + dz + NZ, NZ)}

    sibling = {"dp": 1 - core}
    partners = (
        [at(dx=k) for k in range(1, NX)] + [at(dy=k) for k in range(1, NY)] + [at(dz=k) for k in range(1, NZ)] + [sibling]
    )

    def send(src, dst, send_sem, recv_sem, device):
        copy = pltpu.make_async_remote_copy(
            src_ref=src, dst_ref=dst, send_sem=send_sem, recv_sem=recv_sem, device_id=device, device_id_type=MESH_ID
        )
        copy.start()

    def wait(ref, sem):
        pltpu.make_async_copy(ref, ref, sem).wait()

    barrier = pltpu.get_barrier_semaphore()
    for device in partners:
        pl.semaphore_signal(barrier, inc=1, device_id=device, device_id_type=MESH_ID)
    loads = [
        pltpu.make_async_copy(src, dst, in_sem.at[k])
        for k, (src, dst) in enumerate(
            [
                (a_hbm, abuf.at[0]), (w_hbm, wbuf.at[:, pl.ds(0, COLS)]), (q_hbm, q_ref), (c_hbm, c_ref),
                (f_hbm, f_ref), (len_hbm, len_ref), (dest_hbm, dest_ref),
            ]
        )
    ]
    for load in loads:
        load.start()
    for load in loads:
        load.wait()
    pl.semaphore_wait(barrier, len(partners))

    def half(item, h):
        return abuf.at[item, pl.ds(pl.multiple_of(h * HALF, HALF), HALF)]

    def send_rows(stream, source, target, h):
        send(half(source, h), half(target, h), a_send.at[stream], a_recv.at[stream, target - 1], at(dy=1 - 2 * stream))

    for i in (0, 1):
        for stream in (0, 1):
            send_rows(stream, 0, i + 1, (i + stream) % 2)

    def gather(i):
        for stream in (0, 1):
            h = (i + stream) % 2
            wait(half(i + 1, h), a_recv.at[stream, i])
            if i < 5:
                send_rows(stream, i + 1, i + 3, h)

    part = [pl.ds(pl.multiple_of(core * (WIDTH // 2) + k * (WIDTH // 4), WIDTH // 4), WIDTH // 4) for k in (0, 1)]
    away = pl.multiple_of((1 - core) * (WIDTH // 2), WIDTH // 2)
    others = [pl.ds(pl.multiple_of(away + k * (WIDTH // 4), WIDTH // 4), WIDTH // 4) for k in (0, 1)]

    def block(rows, j):
        return wbuf.at[rows, pl.ds(j * COLS, COLS)]

    def send_weights(turn):
        for way in (0, 1):
            rows = part[way ^ turn]
            send(block(rows, 0), block(rows, 1 + way), w_send.at[0], w_recv.at[way, turn], at(dx=1 - 2 * way))

    def pass_weights(turn):
        for way in (0, 1):
            rows = part[way ^ turn]
            held = block(rows, 1 + way)
            wait(held, w_recv.at[way, turn])
            if turn == 0:
                send(held, block(rows, 3), w_send.at[0], w_recv.at[2, way], at(dx=1 - 2 * way))
            send(held, held, w_send.at[1], w_recv.at[3 + way, turn], sibling)

    def pass_last_weights():
        for way in (0, 1):
            held = block(part[way], 3)
            wait(held, w_recv.at[2, way])
            send(held, held, w_send.at[1], w_recv.at[5, way], sibling)

    def take_weights(way):
        for turn in (0, 1):
            k = way ^ turn if way < 2 else turn
            wait(block(others[k], 1 + way), w_recv.at[3 + way, turn])

    send_weights(0)
    send_weights(1)

    def project(first, items, blocks):
        rows = abuf[first : first + items].reshape(items * BLOCK, WIDTH)
        out = dot(rows, wbuf[:, blocks[0] * COLS : (blocks[-1] + 1) * COLS])
        for m in range(items):
            for j in blocks:
                c = CHUNKS.index((first + m, j))
                for h in (0, 1):
                    pbuf[2 * c + h] = out[
                        m * BLOCK + h * HALF : m * BLOCK + (h + 1) * HALF,
                        (j - blocks[0]) * COLS : (j - blocks[0] + 1) * COLS,
                    ]

    up = 1 - 2 * core

    def piece(r, far):
        return pbuf[8 * r + lax.rem(z + far + NZ, NZ)]

    def stage(r, t):
        for side in (0, 1):
            if side > t:
                continue
            way = up if side == 0 else -up
            at_slot, from_slot = 4 * side + t - side, 4 * side + t - side - 1
            total = piece(r, way * (4 - t))
            if t > side:
                wait(rbuf.at[r, from_slot], c_recv.at[r, from_slot])
                total = total + rbuf[r, from_slot].astype(F32)
            sbuf[r, at_slot] = total.astype(BF16)
            send(sbuf.at[r, at_slot], rbuf.at[r, at_slot], c_send.at[0], c_recv.at[r, at_slot], at(dz=way))

    own_half, own_chunk = lax.rem(z, 2), z // 2

    def pick(values):
        out = values[3]
        for k in range(3):
            out = jnp.where(own_chunk == k, values[k], out)
        return out

    def spot(m, h):
        steps = (m + 1) // 2
        sign = jnp.where(lax.rem(m + h, 2) == 0, 1, -1)
        return lax.rem(y + sign * steps + 2 * NY, NY)

    def shift(j):
        return jnp.where(j == 1, NX - 1, jnp.where(j == 0, 0, j - 1))

    def out_rows(item_y, h):
        return rec_ref.at[pl.ds(pl.multiple_of(lax.rem(item_y, 4) * BLOCK + h * HALF, HALF), HALF)]

    def keep(src, rows):
        pltpu.make_async_copy(src, rows, out_recv.at[0]).start()

    def finish(r):
        total = piece(r, 0)
        for slot in (3, 6):
            wait(rbuf.at[r, slot], c_recv.at[r, slot])
            total = total + rbuf[r, slot].astype(F32)
        sbuf[r, 7] = total.astype(BF16)
        j = pick([c[1] for c in CHUNKS[4 * r : 4 * r + 4]])

        @pl.when(j == 0)
        def _():
            pltpu.make_async_copy(sbuf.at[r, 7], moved.at[r], m_recv.at[r]).start()

        @pl.when(j > 0)
        def _():
            send(sbuf.at[r, 7], moved.at[r], m_send.at[r], m_recv.at[r], at(dx=shift(j)))

    def home(r):
        chunks = CHUNKS[4 * r : 4 * r + 4]
        item_y = spot(pick([c[0] for c in chunks]), own_half)
        from_x = lax.rem(x - shift(pick([c[1] for c in chunks])) + NX, NX)
        return out_rows(item_y, own_half), 2 * from_x + item_y // 4

    def deliver(r):
        wait(moved.at[r], m_recv.at[r])
        rows, to_z = home(r)

        @pl.when(to_z == z)
        def _():
            keep(moved.at[r], rows)

        @pl.when(to_z != z)
        def _():
            send(moved.at[r], rows, f_send.at[r], out_recv.at[0], at(dz=to_z - z))

    def exchange(r):
        e = r - LATE
        for j in range(NX):
            for h in (0, 1):
                part_sum = pbuf[8 * r + 2 * j + h].astype(BF16)
                if j == 0:
                    xr[e, 0, h] = part_sum
                else:
                    xs[e, j - 1, h] = part_sum
            if j > 0:
                send(xs.at[e, j - 1], xr.at[e, j], x_send.at[e, j - 1], x_recv.at[e, j - 1], at(dx=(0, 3, 1, 2)[j]))

    def exchanged(r):
        for j in range(1, NX):
            wait(xr.at[r - LATE, j], x_recv.at[r - LATE, j - 1])

    def late_messages(r, t, act):
        for k, (turn, side, far, hop, after) in enumerate(HOPS[r]):
            if turn == t:
                way = up if side == 0 else -up
                q = lax.rem(z + way * far + NZ, NZ)
                for h in (0, 1):
                    pl.when(spot(r, h) // 4 == lax.rem(q, 2))(
                        functools.partial(act, r - LATE, k, after, way * hop, q, h)
                    )

    def late_piece(e, q, h):
        away = lax.rem(x - q // 2 + NX, NX)
        j = jnp.where(away == 0, 0, jnp.where(away == 3, 1, away + 1))
        return xr[e, j, h].astype(F32)

    def late_send(e, k, after, dz, q, h):
        total = late_piece(e, q, h)
        if after is not None:
            wait(lr.at[e, after, h], l_recv.at[e, after, h])
            total = total + lr[e, after, h].astype(F32)
        ls[e, k, h] = total.astype(BF16)
        send(ls.at[e, k, h], lr.at[e, k, h], l_send.at[e, k, h], l_recv.at[e, k, h], at(dz=dz))

    def late_drain(e, k, after, dz, q, h):
        wait(ls.at[e, k, h], l_send.at[e, k, h])

    def late_finish(r):
        e = r - LATE
        ends = [k for k in range(NZ - 1) if k not in [hop[4] for hop in HOPS[r]]]
        for h in (0, 1):
            item_y = spot(r, h)

            @pl.when(item_y // 4 == lax.rem(z, 2))
            def _():
                total = late_piece(e, z, h)
                for k in ends:
                    wait(lr.at[e, k, h], l_recv.at[e, k, h])
                    total = total + lr[e, k, h].astype(F32)
                ls[e, 7, h] = total.astype(BF16)
                keep(ls.at[e, 7, h], out_rows(item_y, h))

    def make_context():
        cbuf[y] = attend(q_ref, f_ref, c_ref, len_ref)

    def send_context():
        for k in range(1, NY):
            send(cbuf.at[y], cbuf.at[y], d_send.at[0], d_recv.at[0], at(dy=k))

    def project_decode():
        wait(cbuf.at[pl.ds(0, NY - 1)], d_recv.at[0])
        rows = cbuf[...].reshape(NY * 16, 512)
        low = dot(rows, wbuf[0:512]).reshape(NY, 16, NX * COLS)
        high = dot(rows, wbuf[512:1024]).reshape(NY, 16, NX * COLS)
        terms = (low[:, :8] + high[:, 8:]).reshape(2, 32, NX * COLS)
        here = pl.ds(2 * x, 2)
        zs[here] = terms[:, :, 0:COLS].astype(BF16)
        for j in range(1, NX):
            xd[j - 1] = terms[:, :, j * COLS : (j + 1) * COLS].astype(BF16)
            send(xd.at[j - 1], zs.at[here], d_send.at[1], d_recv.at[1], at(dx=(0, 3, 1, 2)[j]))

    def spread_decode():
        wait(zs.at[pl.ds(0, 6)], d_recv.at[1])
        zr[z] = zs[z]
        for k in range(1, NZ):
            send(zs.at[lax.rem(z + k, NZ)], zr.at[z], d_send.at[2], d_recv.at[2], at(dz=k))

    def hand_over():
        wait(zr.at[pl.ds(0, NZ - 1)], d_recv.at[2])
        total = zr[0].astype(F32)
        for k in range(1, NZ):
            total = total + zr[k].astype(F32)
        decoded = total.astype(BF16)
        dec_ref[...] = decoded
        maps = placement(dest_ref)
        out = dot(maps[0], decoded[:, :128]) + dot(maps[1], decoded[:, 128:])
        h1s[...] = out.astype(BF16).reshape(NY, 16, 128)
        h1r[y] = h1s[y]
        for k in range(1, NY):
            send(h1s.at[lax.rem(y + k, NY)], h1r.at[y], d_send.at[3], d_recv.at[3], at(dy=k))

    def hand_on():
        wait(h1r.at[pl.ds(0, NY - 1)], d_recv.at[3])
        h2s[...] = dot(regroup(), h1r[...].reshape(128, 128)).astype(BF16).reshape(NX, 32, 128)
        h2r[x] = h2s[x]
        for k in range(1, NX):
            send(h2s.at[lax.rem(x + k, NX)], h2r.at[x], d_send.at[4], d_recv.at[4], at(dx=k))

    def take():
        wait(h2r.at[pl.ds(0, NX - 1)], d_recv.at[4])
        out = dot(regroup_last(), h2r[...].reshape(128, 128))
        hand_ref[0, 0, 0] = jnp.concatenate([out[2 * k : 2 * k + 2] for k in range(64)], axis=1).astype(BF16)

    tasks = {
        "ctx": make_context, "cs": send_context, "pd": project_decode, "sd": spread_decode, "ho": hand_over, "hon": hand_on, "take": take,
        "g": gather, "pw": pass_weights, "plw": pass_last_weights, "tw": take_weights,
        "pA": lambda: project(0, 3, (0,)), "pB": lambda: project(0, 3, (1, 2)), "pC": lambda: project(3, 1, (0, 1, 2)),
        "pD": lambda: project(0, 4, (3,)), "p": lambda m: project(m, 1, range(NX)),
        "x": exchange, "e": exchanged, "s": stage, "f": finish, "d": deliver,
        "l": lambda r, t: late_messages(r, t, late_send), "F": late_finish,
    }
    for name, *numbers in ORDER:
        tasks[name](*numbers)

    wait(rec_ref, out_recv.at[0])
    for r in range(LATE):
        @pl.when(pick([c[1] for c in CHUNKS[4 * r : 4 * r + 4]]) > 0)
        def _():
            wait(sbuf.at[r, 7], m_send.at[r])

        @pl.when(home(r)[1] != z)
        def _():
            wait(moved.at[r], f_send.at[r])

    for r in range(LATE, ROUNDS):
        for t in range(4):
            late_messages(r, t, late_drain)
        for j in range(NX - 1):
            wait(xs.at[r - LATE, j], x_send.at[r - LATE, j])
    wait(sbuf.at[:, pl.ds(0, 7)], c_send.at[0])
    for h in (0, 1):
        wait(abuf.at[pl.ds(0, 7), pl.ds(0, HALF)], a_send.at[h])
    wait(wbuf.at[pl.ds(0, 512), pl.ds(0, 3 * COLS)], w_send.at[0])
    wait(wbuf.at[pl.ds(0, 512), pl.ds(0, 3 * COLS)], w_send.at[1])
    wait(cbuf.at[pl.ds(0, NY - 1)], d_send.at[0])
    wait(xd, d_send.at[1])
    wait(zs.at[pl.ds(0, NZ - 1)], d_send.at[2])
    wait(h1s.at[pl.ds(0, NY - 1)], d_send.at[3])
    wait(h2s.at[pl.ds(0, NX - 1)], d_send.at[4])


def emit(*refs):
    given, out, held, sems = refs[:3], refs[3:6], refs[6:9], refs[9]
    loads = [pltpu.make_async_copy(given[k], held[k], sems.at[0, k]) for k in range(3)]
    stores = [pltpu.make_async_copy(held[k], out[k], sems.at[1, k]) for k in range(3)]
    for load in loads:
        load.start()
    for load, store in zip(loads, stores):
        load.wait()
        store.start()
    for store in stores:
        store.wait()


def local(query, fresh_key_value, cache, lengths, destination, out_weight, learner_ctx):
    vmem = pl.BlockSpec(memory_space=pltpu.VMEM)
    dma = pltpu.SemaphoreType.DMA
    results = pl.pallas_call(
        kernel,
        out_shape=(
            jax.ShapeDtypeStruct((32, COLS), BF16),
            jax.ShapeDtypeStruct((1, 1, 1, 2, 8192), BF16),
            jax.ShapeDtypeStruct((512, COLS), BF16),
        ),
        in_specs=[pl.BlockSpec(memory_space=pltpu.HBM)] * 7,
        out_specs=(vmem, vmem, pl.BlockSpec(memory_space=pltpu.HBM)),
        scratch_shapes=[
            pltpu.VMEM((8, WIDTH), BF16),
            pltpu.VMEM((16, HEAD_SIZE), BF16),
            pltpu.VMEM((8, 2 * CACHED_POSITIONS, HEAD_SIZE), BF16),
            pltpu.SMEM((8,), jnp.int32),
            pltpu.VMEM((1, 32), jnp.int32),
            pltpu.VMEM((ITEMS, BLOCK, WIDTH), BF16),
            pltpu.VMEM((WIDTH, NX * COLS), BF16),
            pltpu.VMEM((ROUNDS * NZ, HALF, COLS), F32),
            pltpu.VMEM((LATE, NZ - 1, HALF, COLS), BF16),
            pltpu.VMEM((LATE, NZ, HALF, COLS), BF16),
            pltpu.VMEM((LATE, HALF, COLS), BF16),
            pltpu.VMEM((ROUNDS - LATE, NX - 1, 2, HALF, COLS), BF16),
            pltpu.VMEM((ROUNDS - LATE, NX, 2, HALF, COLS), BF16),
            pltpu.VMEM((ROUNDS - LATE, NZ, 2, HALF, COLS), BF16),
            pltpu.VMEM((ROUNDS - LATE, NZ - 1, 2, HALF, COLS), BF16),
            pltpu.VMEM((NY, 16, 512), BF16),
            pltpu.VMEM((NX - 1, 2, 32, COLS), BF16),
            pltpu.VMEM((NZ, 32, COLS), BF16),
            pltpu.VMEM((NZ, 32, COLS), BF16),
            pltpu.VMEM((NY, 16, 128), BF16),
            pltpu.VMEM((NY, 16, 128), BF16),
            pltpu.VMEM((NX, 32, 128), BF16),
            pltpu.VMEM((NX, 32, 128), BF16),
            dma((7,)),
            dma((2,)),
            dma((2, 7)),
            dma((2,)),
            dma((6, 2)),
            dma((5,)),
            dma((5,)),
            dma((1,)),
            dma((LATE, NZ - 1)),
            dma((LATE,)),
            dma((LATE,)),
            dma((LATE,)),
            dma((ROUNDS - LATE, NX - 1)),
            dma((ROUNDS - LATE, NX - 1)),
            dma((ROUNDS - LATE, NZ - 1, 2)),
            dma((ROUNDS - LATE, NZ - 1, 2)),
            dma((1,)),
        ],
        compiler_params=pltpu.CompilerParams(
            collective_id=0, has_side_effects=True, vmem_limit_bytes=63 * 1024 * 1024
        ),
        cost_estimate=pl.CostEstimate(flops=2300000000, bytes_accessed=2500000, transcendentals=33000),
        name="project",
    )(
        query,
        fresh_key_value.reshape(16, HEAD_SIZE),
        cache.reshape(8, 2 * CACHED_POSITIONS, HEAD_SIZE),
        lengths,
        destination.reshape(1, 32),
        out_weight,
        learner_ctx,
    )
    in_hbm = pl.BlockSpec(memory_space=pltpu.HBM)
    return pl.pallas_call(
        emit,
        out_shape=tuple(jax.ShapeDtypeStruct(r.shape, r.dtype) for r in results),
        in_specs=[in_hbm] * 3,
        out_specs=(in_hbm,) * 3,
        scratch_shapes=[pltpu.VMEM(r.shape, r.dtype) for r in results] + [dma((2, 3))],
        compiler_params=pltpu.CompilerParams(vmem_limit_bytes=63 * 1024 * 1024),
        name="emit",
    )(*results)


def solution(mesh):
    return jax.shard_map(
        local,
        mesh=mesh,
        in_specs=(
            P(("dp", "seq"), "tensor"),
            P(("dp", "seq"), None, "tensor"),
            P(("dp", "seq"), None, None, "tensor"),
            P(("dp", "seq")),
            P(("dp", "tensor"), None),
            P("tensor", "seq"),
            P(("dp", "seq"), "tensor"),
        ),
        out_specs=(
            P(("dp", "tensor"), "seq"),
            P("dp", "seq", "tensor", None, None),
            P(("dp", "tensor"), "seq"),
        ),
        check_vma=False,
    )
```

```python
import functools

import jax
import jax.numpy as jnp
from jax import lax
from jax.experimental import pallas as pl
from jax.experimental.pallas import tpu as pltpu
from jax.sharding import PartitionSpec as P

QUERY_GROUP = 8
HEAD_SIZE = 128
CACHED_POSITIONS = 256
NX, NY, NZ = 4, 8, 8
BLOCK = 128
HALF = 64
WIDTH = 1024
COLS = 256
ITEMS = NY
CHUNKS = [(0, 0), (1, 0), (2, 0), (0, 1), (0, 2), (1, 1), (1, 2), (2, 1), (2, 2), (3, 0), (3, 1), (3, 2)]
CHUNKS += [(m, 3) for m in range(4)] + [(m, j) for m in range(4, ITEMS) for j in range(NX)]
ROUNDS, LATE = 8, 4
SHORT_HOPS = [
    (0, 0, 4, 1, None), (0, 1, 3, 1, None), (1, 0, 3, 1, 0), (1, 1, 2, 1, 1), (2, 0, 2, 1, 2), (2, 1, 1, 1, 3),
    (3, 0, 1, 1, 4),
]
HOPS = {r: SHORT_HOPS for r in range(LATE, ROUNDS)}

ORDER = [
    ("ctx",), ("g", 0), ("pw", 0), ("g", 1), ("pw", 1), ("pA",), ("tw", 0), ("tw", 1), ("pB",), ("s", 0, 0),
    ("s", 1, 0), ("g", 2), ("plw",), ("pC",), ("tw", 2), ("pD",), ("s", 2, 0), ("s", 3, 0), ("s", 0, 1), ("s", 1, 1),
    ("g", 3), ("cs",), ("p", 4), ("x", 4), ("s", 2, 1), ("s", 3, 1), ("s", 0, 2), ("s", 1, 2), ("g", 4), ("p", 5),
    ("x", 5), ("e", 4), ("l", 4, 0), ("s", 2, 2), ("s", 3, 2), ("s", 0, 3), ("s", 1, 3), ("g", 5), ("p", 6), ("x", 6),
    ("e", 5), ("l", 5, 0), ("l", 4, 1), ("pd",), ("g", 6), ("p", 7), ("x", 7), ("s", 2, 3), ("s", 3, 3), ("e", 6),
    ("l", 6, 0), ("sd",), ("f", 0), ("f", 1), ("l", 5, 1), ("l", 4, 2), ("e", 7), ("l", 7, 0), ("l", 6, 1), ("ho",),
    ("f", 2), ("f", 3), ("d", 0), ("d", 1), ("l", 5, 2), ("l", 4, 3), ("l", 7, 1), ("l", 6, 2), ("l", 5, 3), ("hon",),
    ("F", 4), ("l", 7, 2), ("l", 6, 3), ("d", 2), ("d", 3), ("F", 5), ("l", 7, 3), ("F", 6), ("take",), ("F", 7),
]
MESH_ID = pl.DeviceIdType.MESH
BF16, F32 = jnp.bfloat16, jnp.float32


def dot(a, b):
    return jnp.dot(a, b, preferred_element_type=F32)


def dot_t(a, b):
    return lax.dot_general(a, b, (((1,), (1,)), ((), ())), preferred_element_type=F32)


def iota(shape, dim):
    return lax.broadcasted_iota(jnp.int32, shape, dim)


def one_hot(condition):
    return jnp.where(condition, 1.0, 0.0).astype(BF16)


def attend(q_ref, f_ref, c_ref, len_ref):
    rows = 8
    by_head = jnp.concatenate(
        [q_ref[:, h * HEAD_SIZE : (h + 1) * HEAD_SIZE].astype(F32) for h in range(QUERY_GROUP)], axis=0
    ).astype(BF16)
    r64, c64 = iota((64, 64), 0), iota((64, 64), 1)
    swap = one_hot((r64 % 8) * 8 + r64 // 8 == c64)
    queries = dot(swap, by_head)
    scale = HEAD_SIZE ** (-0.5)
    scores = []
    place = iota((8, 2 * CACHED_POSITIONS), 1)
    for r in range(rows):
        s = dot_t(queries[r * 8 : (r + 1) * 8].astype(BF16), c_ref[r]) * scale
        valid = (place % 2 == 0) & (place < 2 * len_ref[r])
        scores.append(jnp.where(valid, s, -1e30))
    scores = jnp.concatenate(scores, axis=0)
    fresh = f_ref[...]
    fresh_scores = dot_t(queries.astype(BF16), fresh) * scale
    row16, col16 = iota((64, 16), 0), iota((64, 16), 1)
    own = jnp.sum(jnp.where(col16 == 2 * (row16 // 8), fresh_scores, 0.0), axis=1, keepdims=True)
    top = jnp.maximum(jnp.max(scores, axis=1, keepdims=True), own)
    expd = jnp.exp(scores - top)
    own_exp = jnp.exp(own - top)
    total = jnp.sum(expd, axis=1, keepdims=True) + own_exp
    weights = pltpu.roll(expd / total, 1, 1)
    own_weight = jnp.where(col16 == 2 * (row16 // 8) + 1, own_exp / total, 0.0).astype(BF16)
    context = [dot(weights[r * 8 : (r + 1) * 8].astype(BF16), c_ref[r]) for r in range(rows)]
    context = jnp.concatenate(context, axis=0) + dot(own_weight, fresh)
    context = dot(swap, context.astype(BF16))
    halves = [
        jnp.concatenate([context[h * 8 : (h + 1) * 8] for h in range(g * 4, g * 4 + 4)], axis=1) for g in (0, 1)
    ]
    return jnp.concatenate(halves, axis=0).astype(BF16)


def placement(dest_ref):
    dest = dest_ref[...].astype(F32)
    r32, c32 = iota((32, 32), 0), iota((32, 32), 1)
    across = jnp.broadcast_to(dest, (32, 32))
    down = dot(jnp.where(r32 == c32, across, 0.0).astype(BF16), jnp.ones((32, 32), BF16))
    earlier = one_hot((down == across) & (r32 < c32))
    rank = dot(jnp.ones((128, 32), BF16), earlier)
    q, i = iota((128, 32), 0), iota((128, 32), 1)
    target = ((q // 4) % 4) * NY + q // 16
    slot = (q // 2) % 2
    hit = (jnp.broadcast_to(dest, (128, 32)) == target.astype(F32)) & (rank == slot.astype(F32))
    return [one_hot(hit & (q % 2 == h)) for h in (0, 1)]


def regroup():
    r, c = iota((128, 128), 0), iota((128, 128), 1)
    return one_hot((r // 4 % 8) * 16 + (r // 32) * 4 + r % 4 == c)


def regroup_last():
    r, c = iota((128, 128), 0), iota((128, 128), 1)
    return one_hot((r // 4) * 4 + (r % 2) * 2 + r // 2 % 2 == c)


def kernel(
    q_hbm, f_hbm, c_hbm, len_hbm, dest_hbm, w_hbm, a_hbm,
    dec_ref, hand_ref, rec_ref,
    q_ref, f_ref, c_ref, len_ref, dest_ref,
    abuf, wbuf, pbuf, rbuf, sbuf, moved, xs, xr, ls, lr, cbuf, xd, zs, zr, h1s, h1r, h2s, h2r,
    in_sem, a_send, a_recv, w_send, w_recv, d_send, d_recv, c_send, c_recv, m_send, m_recv, f_send, x_send, x_recv, l_send, l_recv, out_recv,
):
    core, seq, z = lax.axis_index("dp"), lax.axis_index("seq"), lax.axis_index("tensor")
    x, y = seq // NY, seq % NY

    def at(dx=0, dy=0, dz=0):
        return {"seq": lax.rem(x + dx + NX, NX) * NY + lax.rem(y + dy + NY, NY), "tensor": lax.rem(z + dz + NZ, NZ)}

    sibling = {"dp": 1 - core}
    partners = (
        [at(dx=k) for k in range(1, NX)] + [at(dy=k) for k in range(1, NY)] + [at(dz=k) for k in range(1, NZ)] + [sibling]
    )

    def send(src, dst, send_sem, recv_sem, device):
        copy = pltpu.make_async_remote_copy(
            src_ref=src, dst_ref=dst, send_sem=send_sem, recv_sem=recv_sem, device_id=device, device_id_type=MESH_ID
        )
        copy.start()

    def wait(ref, sem):
        pltpu.make_async_copy(ref, ref, sem).wait()

    barrier = pltpu.get_barrier_semaphore()
    for device in partners:
        pl.semaphore_signal(barrier, inc=1, device_id=device, device_id_type=MESH_ID)
    loads = [
        pltpu.make_async_copy(src, dst, in_sem.at[k])
        for k, (src, dst) in enumerate(
            [
                (a_hbm, abuf.at[0]), (w_hbm, wbuf.at[:, pl.ds(0, COLS)]), (q_hbm, q_ref), (c_hbm, c_ref),
                (f_hbm, f_ref), (len_hbm, len_ref), (dest_hbm, dest_ref),
            ]
        )
    ]
    for load in loads:
        load.start()
    for load in loads[:2]:
        load.wait()
    pl.semaphore_wait(barrier, len(partners))

    def half(item, h):
        return abuf.at[item, pl.ds(pl.multiple_of(h * HALF, HALF), HALF)]

    def send_rows(stream, source, target, h):
        send(half(source, h), half(target, h), a_send.at[stream], a_recv.at[stream, target - 1], at(dy=1 - 2 * stream))

    for i in (0, 1):
        for stream in (0, 1):
            send_rows(stream, 0, i + 1, (i + stream) % 2)

    def gather(i):
        for stream in (0, 1):
            h = (i + stream) % 2
            wait(half(i + 1, h), a_recv.at[stream, i])
            if i < 5:
                send_rows(stream, i + 1, i + 3, h)

    part = [pl.ds(pl.multiple_of(core * (WIDTH // 2) + k * (WIDTH // 4), WIDTH // 4), WIDTH // 4) for k in (0, 1)]
    away = pl.multiple_of((1 - core) * (WIDTH // 2), WIDTH // 2)
    others = [pl.ds(pl.multiple_of(away + k * (WIDTH // 4), WIDTH // 4), WIDTH // 4) for k in (0, 1)]

    def block(rows, j):
        return wbuf.at[rows, pl.ds(j * COLS, COLS)]

    def send_weights(turn):
        for way in (0, 1):
            rows = part[way ^ turn]
            send(block(rows, 0), block(rows, 1 + way), w_send.at[0], w_recv.at[way, turn], at(dx=1 - 2 * way))

    def pass_weights(turn):
        for way in (0, 1):
            rows = part[way ^ turn]
            held = block(rows, 1 + way)
            wait(held, w_recv.at[way, turn])
            if turn == 0:
                send(held, block(rows, 3), w_send.at[0], w_recv.at[2, way], at(dx=1 - 2 * way))
            send(held, held, w_send.at[1], w_recv.at[3 + way, turn], sibling)

    def pass_last_weights():
        for way in (0, 1):
            held = block(part[way], 3)
            wait(held, w_recv.at[2, way])
            send(held, held, w_send.at[1], w_recv.at[5, way], sibling)

    def take_weights(way):
        for turn in (0, 1):
            k = way ^ turn if way < 2 else turn
            wait(block(others[k], 1 + way), w_recv.at[3 + way, turn])

    send_weights(0)
    send_weights(1)

    def project(first, items, blocks):
        rows = abuf[first : first + items].reshape(items * BLOCK, WIDTH)
        out = dot(rows, wbuf[:, blocks[0] * COLS : (blocks[-1] + 1) * COLS])
        for m in range(items):
            for j in blocks:
                c = CHUNKS.index((first + m, j))
                for h in (0, 1):
                    pbuf[2 * c + h] = out[
                        m * BLOCK + h * HALF : m * BLOCK + (h + 1) * HALF,
                        (j - blocks[0]) * COLS : (j - blocks[0] + 1) * COLS,
                    ]

    up = 1 - 2 * core

    def piece(r, far):
        return pbuf[8 * r + lax.rem(z + far + NZ, NZ)]

    def stage(r, t):
        for side in (0, 1):
            if side > t:
                continue
            way = up if side == 0 else -up
            at_slot, from_slot = 4 * side + t - side, 4 * side + t - side - 1
            total = piece(r, way * (4 - t))
            if t > side:
                wait(rbuf.at[r, from_slot], c_recv.at[r, from_slot])
                total = total + rbuf[r, from_slot].astype(F32)
            sbuf[r, at_slot] = total.astype(BF16)
            send(sbuf.at[r, at_slot], rbuf.at[r, at_slot], c_send.at[0], c_recv.at[r, at_slot], at(dz=way))

    own_half, own_chunk = lax.rem(z, 2), z // 2

    def pick(values):
        out = values[3]
        for k in range(3):
            out = jnp.where(own_chunk == k, values[k], out)
        return out

    def spot(m, h):
        steps = (m + 1) // 2
        sign = jnp.where(lax.rem(m + h, 2) == 0, 1, -1)
        return lax.rem(y + sign * steps + 2 * NY, NY)

    def shift(j):
        return jnp.where(j == 1, NX - 1, jnp.where(j == 0, 0, j - 1))

    def out_rows(item_y, h):
        return rec_ref.at[pl.ds(pl.multiple_of(lax.rem(item_y, 4) * BLOCK + h * HALF, HALF), HALF)]

    def keep(src, rows):
        pltpu.make_async_copy(src, rows, out_recv.at[0]).start()

    def finish(r):
        total = piece(r, 0)
        for slot in (3, 6):
            wait(rbuf.at[r, slot], c_recv.at[r, slot])
            total = total + rbuf[r, slot].astype(F32)
        sbuf[r, 7] = total.astype(BF16)
        j = pick([c[1] for c in CHUNKS[4 * r : 4 * r + 4]])

        @pl.when(j == 0)
        def _():
            pltpu.make_async_copy(sbuf.at[r, 7], moved.at[r], m_recv.at[r]).start()

        @pl.when(j > 0)
        def _():
            send(sbuf.at[r, 7], moved.at[r], m_send.at[r], m_recv.at[r], at(dx=shift(j)))

    def home(r):
        chunks = CHUNKS[4 * r : 4 * r + 4]
        item_y = spot(pick([c[0] for c in chunks]), own_half)
        from_x = lax.rem(x - shift(pick([c[1] for c in chunks])) + NX, NX)
        return out_rows(item_y, own_half), 2 * from_x + item_y // 4

    def deliver(r):
        wait(moved.at[r], m_recv.at[r])
        rows, to_z = home(r)

        @pl.when(to_z == z)
        def _():
            keep(moved.at[r], rows)

        @pl.when(to_z != z)
        def _():
            send(moved.at[r], rows, f_send.at[r], out_recv.at[0], at(dz=to_z - z))

    def exchange(r):
        e = r - LATE
        for j in range(NX):
            for h in (0, 1):
                part_sum = pbuf[8 * r + 2 * j + h].astype(BF16)
                if j == 0:
                    xr[e, 0, h] = part_sum
                else:
                    xs[e, j - 1, h] = part_sum
            if j > 0:
                send(xs.at[e, j - 1], xr.at[e, j], x_send.at[e, j - 1], x_recv.at[e, j - 1], at(dx=(0, 3, 1, 2)[j]))

    def exchanged(r):
        for j in range(1, NX):
            wait(xr.at[r - LATE, j], x_recv.at[r - LATE, j - 1])

    def late_messages(r, t, act):
        for k, (turn, side, far, hop, after) in enumerate(HOPS[r]):
            if turn == t:
                way = up if side == 0 else -up
                q = lax.rem(z + way * far + NZ, NZ)
                for h in (0, 1):
                    pl.when(spot(r, h) // 4 == lax.rem(q, 2))(
                        functools.partial(act, r - LATE, k, after, way * hop, q, h)
                    )

    def late_piece(e, q, h):
        away = lax.rem(x - q // 2 + NX, NX)
        j = jnp.where(away == 0, 0, jnp.where(away == 3, 1, away + 1))
        return xr[e, j, h].astype(F32)

    def late_send(e, k, after, dz, q, h):
        total = late_piece(e, q, h)
        if after is not None:
            wait(lr.at[e, after, h], l_recv.at[e, after, h])
            total = total + lr[e, after, h].astype(F32)
        ls[e, k, h] = total.astype(BF16)
        send(ls.at[e, k, h], lr.at[e, k, h], l_send.at[e, k, h], l_recv.at[e, k, h], at(dz=dz))

    def late_drain(e, k, after, dz, q, h):
        wait(ls.at[e, k, h], l_send.at[e, k, h])

    def late_finish(r):
        e = r - LATE
        ends = [k for k in range(NZ - 1) if k not in [hop[4] for hop in HOPS[r]]]
        for h in (0, 1):
            item_y = spot(r, h)

            @pl.when(item_y // 4 == lax.rem(z, 2))
            def _():
                total = late_piece(e, z, h)
                for k in ends:
                    wait(lr.at[e, k, h], l_recv.at[e, k, h])
                    total = total + lr[e, k, h].astype(F32)
                ls[e, 7, h] = total.astype(BF16)
                keep(ls.at[e, 7, h], out_rows(item_y, h))

    def make_context():
        for load in loads[2:]:
            load.wait()
        cbuf[y] = attend(q_ref, f_ref, c_ref, len_ref)

    def send_context():
        for k in range(1, NY):
            send(cbuf.at[y], cbuf.at[y], d_send.at[0], d_recv.at[0], at(dy=k))

    def project_decode():
        wait(cbuf.at[pl.ds(0, NY - 1)], d_recv.at[0])
        rows = cbuf[...].reshape(NY * 16, 512)
        low = dot(rows, wbuf[0:512]).reshape(NY, 16, NX * COLS)
        high = dot(rows, wbuf[512:1024]).reshape(NY, 16, NX * COLS)
        terms = (low[:, :8] + high[:, 8:]).reshape(2, 32, NX * COLS)
        here = pl.ds(2 * x, 2)
        zs[here] = terms[:, :, 0:COLS].astype(BF16)
        for j in range(1, NX):
            xd[j - 1] = terms[:, :, j * COLS : (j + 1) * COLS].astype(BF16)
            send(xd.at[j - 1], zs.at[here], d_send.at[1], d_recv.at[1], at(dx=(0, 3, 1, 2)[j]))

    def spread_decode():
        wait(zs.at[pl.ds(0, 6)], d_recv.at[1])
        zr[z] = zs[z]
        for k in range(1, NZ):
            send(zs.at[lax.rem(z + k, NZ)], zr.at[z], d_send.at[2], d_recv.at[2], at(dz=k))

    def hand_over():
        wait(zr.at[pl.ds(0, NZ - 1)], d_recv.at[2])
        total = zr[0].astype(F32)
        for k in range(1, NZ):
            total = total + zr[k].astype(F32)
        decoded = total.astype(BF16)
        dec_ref[...] = decoded
        maps = placement(dest_ref)
        out = dot(maps[0], decoded[:, :128]) + dot(maps[1], decoded[:, 128:])
        h1s[...] = out.astype(BF16).reshape(NY, 16, 128)
        h1r[y] = h1s[y]
        for k in range(1, NY):
            send(h1s.at[lax.rem(y + k, NY)], h1r.at[y], d_send.at[3], d_recv.at[3], at(dy=k))

    def hand_on():
        wait(h1r.at[pl.ds(0, NY - 1)], d_recv.at[3])
        h2s[...] = dot(regroup(), h1r[...].reshape(128, 128)).astype(BF16).reshape(NX, 32, 128)
        h2r[x] = h2s[x]
        for k in range(1, NX):
            send(h2s.at[lax.rem(x + k, NX)], h2r.at[x], d_send.at[4], d_recv.at[4], at(dx=k))

    def take():
        wait(h2r.at[pl.ds(0, NX - 1)], d_recv.at[4])
        out = dot(regroup_last(), h2r[...].reshape(128, 128))
        hand_ref[0, 0, 0] = jnp.concatenate([out[2 * k : 2 * k + 2] for k in range(64)], axis=1).astype(BF16)

    tasks = {
        "ctx": make_context, "cs": send_context, "pd": project_decode, "sd": spread_decode, "ho": hand_over, "hon": hand_on, "take": take,
        "g": gather, "pw": pass_weights, "plw": pass_last_weights, "tw": take_weights,
        "pA": lambda: project(0, 3, (0,)), "pB": lambda: project(0, 3, (1, 2)), "pC": lambda: project(3, 1, (0, 1, 2)),
        "pD": lambda: project(0, 4, (3,)), "p": lambda m: project(m, 1, range(NX)),
        "x": exchange, "e": exchanged, "s": stage, "f": finish, "d": deliver,
        "l": lambda r, t: late_messages(r, t, late_send), "F": late_finish,
    }
    for name, *numbers in ORDER:
        tasks[name](*numbers)

    wait(rec_ref, out_recv.at[0])
    for r in range(LATE):
        @pl.when(pick([c[1] for c in CHUNKS[4 * r : 4 * r + 4]]) > 0)
        def _():
            wait(sbuf.at[r, 7], m_send.at[r])

        @pl.when(home(r)[1] != z)
        def _():
            wait(moved.at[r], f_send.at[r])

    for r in range(LATE, ROUNDS):
        for t in range(4):
            late_messages(r, t, late_drain)
        for j in range(NX - 1):
            wait(xs.at[r - LATE, j], x_send.at[r - LATE, j])
    wait(sbuf.at[:, pl.ds(0, 7)], c_send.at[0])
    for h in (0, 1):
        wait(abuf.at[pl.ds(0, 7), pl.ds(0, HALF)], a_send.at[h])
    wait(wbuf.at[pl.ds(0, 512), pl.ds(0, 3 * COLS)], w_send.at[0])
    wait(wbuf.at[pl.ds(0, 512), pl.ds(0, 3 * COLS)], w_send.at[1])
    wait(cbuf.at[pl.ds(0, NY - 1)], d_send.at[0])
    wait(xd, d_send.at[1])
    wait(zs.at[pl.ds(0, NZ - 1)], d_send.at[2])
    wait(h1s.at[pl.ds(0, NY - 1)], d_send.at[3])
    wait(h2s.at[pl.ds(0, NX - 1)], d_send.at[4])


def emit(*refs):
    given, out, held, sems = refs[:3], refs[3:6], refs[6:9], refs[9]
    loads = [pltpu.make_async_copy(given[k], held[k], sems.at[0, k]) for k in range(3)]
    stores = [pltpu.make_async_copy(held[k], out[k], sems.at[1, k]) for k in range(3)]
    for load in loads:
        load.start()
    for load, store in zip(loads, stores):
        load.wait()
        store.start()
    for store in stores:
        store.wait()


def local(query, fresh_key_value, cache, lengths, destination, out_weight, learner_ctx):
    vmem = pl.BlockSpec(memory_space=pltpu.VMEM)
    dma = pltpu.SemaphoreType.DMA
    results = pl.pallas_call(
        kernel,
        out_shape=(
            jax.ShapeDtypeStruct((32, COLS), BF16),
            jax.ShapeDtypeStruct((1, 1, 1, 2, 8192), BF16),
            jax.ShapeDtypeStruct((512, COLS), BF16),
        ),
        in_specs=[pl.BlockSpec(memory_space=pltpu.HBM)] * 7,
        out_specs=(vmem, vmem, pl.BlockSpec(memory_space=pltpu.HBM)),
        scratch_shapes=[
            pltpu.VMEM((8, WIDTH), BF16),
            pltpu.VMEM((16, HEAD_SIZE), BF16),
            pltpu.VMEM((8, 2 * CACHED_POSITIONS, HEAD_SIZE), BF16),
            pltpu.SMEM((8,), jnp.int32),
            pltpu.VMEM((1, 32), jnp.int32),
            pltpu.VMEM((ITEMS, BLOCK, WIDTH), BF16),
            pltpu.VMEM((WIDTH, NX * COLS), BF16),
            pltpu.VMEM((ROUNDS * NZ, HALF, COLS), F32),
            pltpu.VMEM((LATE, NZ - 1, HALF, COLS), BF16),
            pltpu.VMEM((LATE, NZ, HALF, COLS), BF16),
            pltpu.VMEM((LATE, HALF, COLS), BF16),
            pltpu.VMEM((ROUNDS - LATE, NX - 1, 2, HALF, COLS), BF16),
            pltpu.VMEM((ROUNDS - LATE, NX, 2, HALF, COLS), BF16),
            pltpu.VMEM((ROUNDS - LATE, NZ, 2, HALF, COLS), BF16),
            pltpu.VMEM((ROUNDS - LATE, NZ - 1, 2, HALF, COLS), BF16),
            pltpu.VMEM((NY, 16, 512), BF16),
            pltpu.VMEM((NX - 1, 2, 32, COLS), BF16),
            pltpu.VMEM((NZ, 32, COLS), BF16),
            pltpu.VMEM((NZ, 32, COLS), BF16),
            pltpu.VMEM((NY, 16, 128), BF16),
            pltpu.VMEM((NY, 16, 128), BF16),
            pltpu.VMEM((NX, 32, 128), BF16),
            pltpu.VMEM((NX, 32, 128), BF16),
            dma((7,)),
            dma((2,)),
            dma((2, 7)),
            dma((2,)),
            dma((6, 2)),
            dma((5,)),
            dma((5,)),
            dma((1,)),
            dma((LATE, NZ - 1)),
            dma((LATE,)),
            dma((LATE,)),
            dma((LATE,)),
            dma((ROUNDS - LATE, NX - 1)),
            dma((ROUNDS - LATE, NX - 1)),
            dma((ROUNDS - LATE, NZ - 1, 2)),
            dma((ROUNDS - LATE, NZ - 1, 2)),
            dma((1,)),
        ],
        compiler_params=pltpu.CompilerParams(
            collective_id=0, has_side_effects=True, vmem_limit_bytes=63 * 1024 * 1024
        ),
        cost_estimate=pl.CostEstimate(flops=2300000000, bytes_accessed=2500000, transcendentals=33000),
        name="project",
    )(
        query,
        fresh_key_value.reshape(16, HEAD_SIZE),
        cache.reshape(8, 2 * CACHED_POSITIONS, HEAD_SIZE),
        lengths,
        destination.reshape(1, 32),
        out_weight,
        learner_ctx,
    )
    in_hbm = pl.BlockSpec(memory_space=pltpu.HBM)
    return pl.pallas_call(
        emit,
        out_shape=tuple(jax.ShapeDtypeStruct(r.shape, r.dtype) for r in results),
        in_specs=[in_hbm] * 3,
        out_specs=(in_hbm,) * 3,
        scratch_shapes=[pltpu.VMEM(r.shape, r.dtype) for r in results] + [dma((2, 3))],
        compiler_params=pltpu.CompilerParams(vmem_limit_bytes=63 * 1024 * 1024),
        name="emit",
    )(*results)


def solution(mesh):
    return jax.shard_map(
        local,
        mesh=mesh,
        in_specs=(
            P(("dp", "seq"), "tensor"),
            P(("dp", "seq"), None, "tensor"),
            P(("dp", "seq"), None, None, "tensor"),
            P(("dp", "seq")),
            P(("dp", "tensor"), None),
            P("tensor", "seq"),
            P(("dp", "seq"), "tensor"),
        ),
        out_specs=(
            P(("dp", "tensor"), "seq"),
            P("dp", "seq", "tensor", None, None),
            P(("dp", "tensor"), "seq"),
        ),
        check_vma=False,
    )
```
